256 devices in a mesh: pipe: 2 (over x_hi), ctx: 32 (over y, z), dp: 4 (over x_lo, core).
Axes of the slice: x: 4 (x_hi: 2, x_lo: 2; x = x_hi * 2 + x_lo), y: 4, z: 8, core: 2. Of those that a mesh axis runs over, the one named last changes fastest.
Arguments:
- queries: bfloat16 [4, 16384, 2048], P('dp', 'ctx', 'pipe'), may hold values from -8 to 8
- keys: bfloat16 [4, 16384, 2048], P('dp', 'ctx', 'pipe'), may hold values from -8 to 8
- values: bfloat16 [4, 16384, 2048], P('dp', 'ctx', 'pipe'), may hold values from -6 to 6
- outputs: bfloat16 [4, 16384, 2048], P('dp', 'ctx', 'pipe'), may hold values from -6 to 6
- out_grads: bfloat16 [4, 16384, 2048], P('dp', 'ctx', 'pipe'), may hold values from -6 to 6
- lengths: int32 [4, 4], P('dp'), may hold values from 1 to 8192, 16384 in all within a row
- proj_weight: bfloat16 [3, 512, 2048], P(None, None, 'pipe'), may hold values from -1.5 to 1.5
- hidden: bfloat16 [4, 32768, 512], P('dp', 'ctx'), may hold values from -0.078125 to 0.078125
- conv_weight: bfloat16 [4, 512, 512], P(None, None, 'pipe'), may hold values from -0.125 to 0.125
Outputs:
- hidden_grad: bfloat16 [4, 32768, 512], P('dp', 'ctx', 'pipe')
- conv_grad: float32 [4, 512, 512], P(None, 'ctx', 'pipe')
The draws below stay inside these ranges and needn't reach their ends.
Inputs may be any that keep to these rules, and one draw needn't show every extreme that they name: Each sequence has 1 to 8192 latent frames, the 4 lengths of a group add up to 16384, and the longest is exactly 8192.
All inputs are finite; a program needn't handle non-finite values.
Results may differ from the reference program's by a relative error of at most 0.0063.
Values may be sent and summed in bfloat16 or wider, within the bound.
A program may use at most 128 MiB of HBM per device.

```python
import math
import jax
import jax.numpy as jnp
import numpy as np
from jax import lax

HEADS = 16
HEAD_DIM = 128
CH = 512
TAPS = 4
SPAN = 1
TOK_DEV = 512
WIDTH = 2048
FRAMES = 16384
MOST = 8192
SEQS = 4
GROUPS = 4
N_CTX = 32


def draw_queries(key, part):
    key = jax.random.fold_in(key, 11)
    result = jnp.clip(jax.random.normal(key, (GROUPS, FRAMES, WIDTH), jnp.float32), -6.0, 6.0)
    return result.astype(jnp.bfloat16)


def draw_keys(key, part):
    key = jax.random.fold_in(key, 23)
    result = jnp.clip(jax.random.normal(key, (GROUPS, FRAMES, WIDTH), jnp.float32), -6.0, 6.0)
    return result.astype(jnp.bfloat16)


def strengthened(array, rng, source, target, parts, factor):
    def block_of(axis_at):
        return (jnp.arange(array.shape[axis_at]) // (array.shape[axis_at] // parts)).reshape((-1,) + (1,) * (array.ndim - 1 - axis_at))

    near = jax.random.permutation(rng, parts)[block_of(target)]
    other_side = (block_of(target) + parts // 2) % parts
    return jnp.where((block_of(source) == near) | (block_of(source) == other_side), factor * array, array)


def steps_of(key, dims, pieces, least, top_value):
    gain = 1.0
    for axis_at, parts in pieces:
        draws = jax.random.uniform(jax.random.fold_in(jax.random.fold_in(key, 6), axis_at), (parts,), jnp.float32, least / len(pieces), top_value / len(pieces))
        gain = gain * jnp.repeat(jnp.exp(draws), dims[axis_at] // parts).reshape((-1,) + (1,) * (len(dims) - 1 - axis_at))
    return gain


def length_profile(number_of, total, most, skew):
    loads = [(1 << 20) // math.isqrt(rank ** skew) + 1 for rank in range(2, number_of + 1)]
    surplus, counts = total - most - (number_of - 1), [1] * (number_of - 1)
    while surplus > 0:
        movable = [i for i in range(number_of - 1) if counts[i] < most]
        whole, left = sum([loads[i] for i in movable]), surplus
        for i in movable:
            more = min(most - counts[i], max(1, left * loads[i] // whole), surplus)
            counts[i] = counts[i] + more
            surplus = surplus - more
    return np.array([most] + counts)


def ragged_sizes(own_key, number_of, total, most, lean):
    if number_of == 2:
        one = jax.random.randint(own_key, (), max(1, total - most), min(most, total - 1) + 1)
        return jnp.stack([one, total - one])
    sizes = jnp.asarray(length_profile(number_of, total, most, lean), jnp.int32)
    couples = (number_of - 1) // 2
    giver, receiver = sizes[1:1 + 2 * couples:2], sizes[2:2 + 2 * couples:2]
    margin = jnp.minimum(giver - 1, most - receiver)
    moved = jax.random.randint(jax.random.fold_in(own_key, 1), (couples,), 0, 1 << 20) % (margin + 1)
    sizes = sizes.at[1:1 + 2 * couples:2].set(giver - moved).at[2:2 + 2 * couples:2].set(receiver + moved)
    return sizes[jax.random.permutation(jax.random.fold_in(own_key, 2), number_of)]


def scatter_about(key, extent, scale, most, pieces=(), kind=jnp.bfloat16):
    array = jax.random.normal(key, extent, jnp.float32) * scale
    if len(pieces) > 0:
        array = steps_of(key, extent, pieces, -0.22, 0.18) * array
    return jnp.clip(array, min=-most, max=most).astype(kind)


def bell_draw_with(own_key, dims, scale, most, cuts, heavy, kind=jnp.bfloat16):
    array = scale * jax.random.normal(own_key, dims, jnp.float32)
    if cuts:
        array = array * steps_of(own_key, dims, cuts, -0.22, 0.18)
    return jnp.clip(strengthened(array, jax.random.fold_in(own_key, 3), *heavy), -most, most).astype(kind)


def setup_inputs(seed: int = 0) -> dict:
    splits = jax.random.split(jax.random.key(seed), 10)
    return {
        "queries": draw_queries(jax.random.fold_in(splits[9], 71), 0),
        "keys": draw_keys(jax.random.fold_in(splits[9], 71), 0),
        "values": scatter_about(splits[2], (GROUPS, FRAMES, WIDTH), 1.0, 6.0, ((0, 4), (1, 32), (2, 2))),
        "outputs": scatter_about(splits[3], (GROUPS, FRAMES, WIDTH), 1.0, 6.0, ((0, 4), (1, 32), (2, 2))),
        "out_grads": scatter_about(splits[4], (GROUPS, FRAMES, WIDTH), 1.0, 6.0, ((0, 4), (1, 32), (2, 2))),
        "lengths": jax.vmap(lambda own: ragged_sizes(own, SEQS, FRAMES, MOST, 2))(jax.random.split(splits[5], GROUPS)).reshape((GROUPS, SEQS)).astype(jnp.int32),
        "proj_weight": scatter_about(splits[6], (3, CH, WIDTH), HEADS ** -0.5, 1.5, ((2, 2),)),
        "hidden": bell_draw_with(splits[7], (GROUPS, 2 * FRAMES, CH), ((2 * FRAMES * GROUPS) ** -0.5), 0.078125, ((0, 4), (1, 32)), (1, 2, 32, 2.75)),
        "conv_weight": scatter_about(splits[8], (TAPS, CH, CH), (TAPS * CH) ** -0.5, 0.125, ((2, 2),)),
    }


masked_score = -1e30
tap_offsets = (-2, -1, -1, 0)


def segment_of(ends, positions):
    counted = jnp.sum((ends[None, :] <= positions[:, None]).astype(jnp.int32), axis=1)
    return jnp.where(positions >= 0, counted, -1).astype(jnp.int32)


def group_attention(query_all, key_all, value_all, output_all, grad_all, ends):
    scale = HEAD_DIM ** -0.5
    reach = SPAN * TOK_DEV
    band = reach + TOK_DEV
    positions = jnp.arange(-reach, FRAMES, dtype=jnp.int32)
    segments = segment_of(ends, positions)
    padding = jnp.zeros((reach, WIDTH), jnp.bfloat16)
    keys_pad = jnp.concatenate([padding, key_all], axis=0)
    values_pad = jnp.concatenate([padding, value_all], axis=0)

    def block_step(carry, block):
        key_acc, value_acc = carry
        start = (block * TOK_DEV).astype(jnp.int32)
        query_rows = lax.dynamic_slice_in_dim(query_all, start, TOK_DEV, 0).astype(jnp.float32)
        output_rows = lax.dynamic_slice_in_dim(output_all, start, TOK_DEV, 0).astype(jnp.float32)
        grad_rows = lax.dynamic_slice_in_dim(grad_all, start, TOK_DEV, 0).astype(jnp.float32)
        key_rows = lax.dynamic_slice_in_dim(keys_pad, start, band, 0).astype(jnp.float32)
        value_rows = lax.dynamic_slice_in_dim(values_pad, start, band, 0).astype(jnp.float32)
        query_heads = query_rows.reshape(TOK_DEV, HEADS, HEAD_DIM)
        output_heads = output_rows.reshape(TOK_DEV, HEADS, HEAD_DIM)
        grad_heads = grad_rows.reshape(TOK_DEV, HEADS, HEAD_DIM)
        key_heads = key_rows.reshape(band, HEADS, HEAD_DIM)
        value_heads = value_rows.reshape(band, HEADS, HEAD_DIM)
        query_pos = start + jnp.arange(TOK_DEV, dtype=jnp.int32)
        key_pos = start - reach + jnp.arange(band, dtype=jnp.int32)
        query_seg = lax.dynamic_slice_in_dim(segments, start + reach, TOK_DEV, 0)
        key_seg = lax.dynamic_slice_in_dim(segments, start, band, 0)
        allowed = (query_seg[:, None] == key_seg[None, :]) & (key_pos[None, :] <= query_pos[:, None]) & (key_seg[None, :] >= 0)
        scores = jnp.einsum("qhd,khd->hqk", query_heads, key_heads) * scale
        row_max = jnp.max(jnp.where(allowed[None], scores, masked_score), axis=-1)
        row_sum = jnp.sum(jnp.where(allowed[None], jnp.exp(scores - row_max[..., None]), 0.0), axis=-1)
        log_total = row_max + jnp.log(row_sum)
        delta = jnp.einsum("qhd,qhd->hq", grad_heads, output_heads)
        prob = jnp.where(allowed[None], jnp.exp(scores - log_total[..., None]), 0.0)
        dprob = jnp.einsum("qhd,khd->hqk", grad_heads, value_heads)
        dscore = lax.optimization_barrier((prob * (dprob - delta[..., None])).astype(jnp.bfloat16)).astype(jnp.float32)
        prob_low = lax.optimization_barrier(prob.astype(jnp.bfloat16)).astype(jnp.float32)
        value_grad = jnp.einsum("hqk,qhd->khd", prob_low, grad_heads)
        key_grad = jnp.einsum("hqk,qhd->khd", dscore, query_heads) * scale
        query_grad = jnp.einsum("hqk,khd->qhd", dscore, key_heads) * scale
        old_keys = lax.dynamic_slice_in_dim(key_acc, start, band, 0)
        old_values = lax.dynamic_slice_in_dim(value_acc, start, band, 0)
        key_acc = lax.dynamic_update_slice_in_dim(key_acc, old_keys + key_grad.reshape(band, WIDTH), start, 0)
        value_acc = lax.dynamic_update_slice_in_dim(value_acc, old_values + value_grad.reshape(band, WIDTH), start, 0)
        return (key_acc, value_acc), query_grad.reshape(TOK_DEV, WIDTH)

    empty = jnp.zeros((FRAMES + reach, WIDTH), jnp.float32)
    carry, query_blocks = lax.scan(block_step, (empty, empty), jnp.arange(N_CTX, dtype=jnp.int32))
    grad_query = query_blocks.reshape(FRAMES, WIDTH).astype(jnp.bfloat16)
    grad_key = carry[0][reach:].astype(jnp.bfloat16)
    grad_value = carry[1][reach:].astype(jnp.bfloat16)
    return grad_query, grad_key, grad_value


def reference(queries, keys, values, outputs, out_grads, lengths, proj_weight, hidden, conv_weight):
    conv_total = jnp.zeros((TAPS, CH, CH), jnp.float32)
    hidden_list = []
    for group in range(GROUPS):
        ends = jnp.cumsum(lengths[group]).astype(jnp.int32)
        grad_query, grad_key, grad_value = group_attention(queries[group], keys[group], values[group], outputs[group], out_grads[group], ends)
        latent = jnp.dot(grad_query, proj_weight[0].T, preferred_element_type=jnp.float32)
        latent = latent + jnp.dot(grad_key, proj_weight[1].T, preferred_element_type=jnp.float32)
        latent = latent + jnp.dot(grad_value, proj_weight[2].T, preferred_element_type=jnp.float32)
        latent = latent.astype(jnp.bfloat16)
        frame_pos = jnp.arange(FRAMES, dtype=jnp.int32)
        frame_seg = segment_of(ends, frame_pos)
        feature_pad = jnp.concatenate([jnp.zeros((4, CH), jnp.bfloat16), hidden[group]], axis=0)
        grad_pad = jnp.zeros((2 * FRAMES + 4, CH), jnp.float32)
        tap_list = []
        for tap in range(TAPS):
            tap_live = segment_of(ends, frame_pos + tap_offsets[tap]) == frame_seg
            features = feature_pad[tap + 1:tap + 1 + 2 * FRAMES:2]
            features = jnp.where(tap_live[:, None], features, jnp.zeros_like(features))
            tap_list.append(jnp.dot(features.T, latent, preferred_element_type=jnp.float32))
            masked_latent = jnp.where(tap_live[:, None], latent, jnp.zeros_like(latent))
            spread = jnp.dot(masked_latent, conv_weight[tap].T, preferred_element_type=jnp.float32)
            grad_pad = grad_pad.at[tap + 1:tap + 1 + 2 * FRAMES:2].add(spread)
        conv_total = conv_total + jnp.stack(tap_list, axis=0)
        hidden_list.append(grad_pad[4:].astype(jnp.bfloat16))
    return jnp.stack(hidden_list, axis=0), conv_total
```

```python
import functools
import jax
import jax.numpy as jnp
from jax import lax
from jax.experimental import pallas as pl
from jax.experimental.pallas import tpu as pltpu
from jax.sharding import PartitionSpec as P

HEAD_DIM = 128
SCALE = HEAD_DIM ** (-0.5)
SCALE_LOG2E = SCALE * 1.4426950408889634
MASKED = -1e30
CHUNKS = 4
MESH = pl.DeviceIdType.MESH
F32 = jnp.float32
BF16 = jnp.bfloat16


def nn(left, right):
    return lax.dot_general(left, right, (((1,), (0,)), ((), ())), preferred_element_type=F32)


def nt(left, right):
    return lax.dot_general(left, right, (((1,), (1,)), ((), ())), preferred_element_type=F32)


def tn(left, right):
    return lax.dot_general(left, right, (((0,), (0,)), ((), ())), preferred_element_type=F32)


def kernel(
    n_ctx,
    lengths,
    q_in,
    k_in,
    v_in,
    o_in,
    g_in,
    w_in,
    hid_in,
    cw_in,
    hid_out,
    conv_out,
    q,
    k,
    v,
    o,
    g,
    w,
    hid,
    cw,
    k_prev,
    v_prev,
    q_next,
    g_next,
    bias_own,
    bias_prev,
    bias_next,
    e_own,
    e_next,
    stat_own,
    stat_next,
    stat_from_next,
    stat_from_prev,
    dq,
    dk,
    dv,
    dk_prev,
    dv_prev,
    dq_next,
    lat_sum,
    back_out,
    back_in,
    fwd_out,
    fwd_in,
    pipe_out,
    pipe_in,
    half_mine,
    half_other,
    ext,
    head_in,
    tail_in,
    taps_mine,
    taps_out,
    taps_in,
    spread,
    conv_part,
    conv_in,
    total,
    local_sem,
    kv_send,
    kv_recv,
    qg_send,
    qg_recv,
    stat_send,
    stat_recv,
    chunk_send,
    chunk_recv,
    misc_send,
    misc_recv,
    rs_send,
    rs_recv,
    dp_send,
    dp_recv,
):
    rows, width = q.shape
    heads = width // HEAD_DIM
    half_heads = heads // 2
    half_width = half_heads * HEAD_DIM
    ch = w.shape[1]
    half = ch // 2
    frames = rows * n_ctx
    share = ch // n_ctx
    chunk = rows // CHUNKS
    pipe = lax.axis_index("pipe")
    ctx = lax.axis_index("ctx")
    dp = lax.axis_index("dp")
    core = lax.rem(dp, 2)
    after = lax.rem(ctx + 1, n_ctx)
    before = lax.rem(ctx + n_ctx - 1, n_ctx)
    other_core = dp + 1 - 2 * core
    start = ctx * rows

    def cols(index):
        return pl.ds(pl.multiple_of(index * HEAD_DIM, HEAD_DIM), HEAD_DIM)

    def remote(src, dst, send, recv, where):
        return pltpu.make_async_remote_copy(
            src_ref=src,
            dst_ref=dst,
            send_sem=send,
            recv_sem=recv,
            device_id=where,
            device_id_type=MESH,
        )

    my_half = pl.ds(pl.multiple_of(pipe * half, half), half)
    their_half = pl.ds(pl.multiple_of((1 - pipe) * half, half), half)
    loads = [
        pltpu.make_async_copy(src, dst, local_sem.at[i])
        for i, (src, dst) in enumerate(
            (
                (hid_in, hid),
                (k_in, k),
                (q_in, q),
                (g_in, g),
                (o_in, o),
                (v_in, v),
                (w_in, w),
                (cw_in.at[:, my_half, :], cw.at[:, :, my_half]),
            )
        )
    ]
    for load in loads:
        load.start()

    barrier = pltpu.get_barrier_semaphore()

    def greet(step, carry):
        pl.semaphore_signal(
            barrier, inc=1, device_id={"ctx": lax.rem(ctx + step, n_ctx)}, device_id_type=MESH
        )
        return carry

    lax.fori_loop(1, n_ctx, greet, 0)
    pl.semaphore_signal(barrier, inc=1, device_id={"pipe": 1 - pipe}, device_id_type=MESH)
    for step in range(1, 4):
        pl.semaphore_signal(
            barrier, inc=1, device_id={"dp": lax.rem(dp + step, 4)}, device_id_type=MESH
        )
    pl.semaphore_wait(barrier, n_ctx - 1 + 1 + 3)

    tail = remote(
        hid_in.at[pl.ds(2 * rows - 16, 16), :],
        tail_in,
        misc_send.at[0],
        misc_recv.at[0],
        {"ctx": after},
    )
    tail.start()

    def kv_copies(index):
        return (
            remote(
                k_in.at[:, cols(index)],
                k_prev.at[:, cols(index)],
                kv_send.at[index, 0],
                kv_recv.at[index, 0],
                {"ctx": after},
            ),
            remote(
                v_in.at[:, cols(index)],
                v_prev.at[:, cols(index)],
                kv_send.at[index, 1],
                kv_recv.at[index, 1],
                {"ctx": after},
            ),
        )

    def qg_copies(index):
        return (
            remote(
                q_in.at[:, cols(half_heads + index)],
                q_next.at[:, cols(index)],
                qg_send.at[index, 0],
                qg_recv.at[index, 0],
                {"ctx": before},
            ),
            remote(
                g_in.at[:, cols(half_heads + index)],
                g_next.at[:, cols(index)],
                qg_send.at[index, 1],
                qg_recv.at[index, 1],
                {"ctx": before},
            ),
        )

    def halo(index, carry):
        for copy in qg_copies(index) + kv_copies(index):
            copy.start()
        return carry

    lax.fori_loop(0, half_heads, halo, 0)
    swap = remote(
        cw_in.at[:, their_half, :],
        cw.at[:, :, my_half],
        misc_send.at[1],
        misc_recv.at[1],
        {"pipe": 1 - pipe},
    )
    swap.start()

    ends = [lengths[0]]
    for i in range(1, 4):
        ends.append(ends[-1] + lengths[i])

    def segment(pos):
        count = jnp.zeros(pos.shape, jnp.int32)
        for end in ends:
            count = count + jnp.where(pos >= end, 1, 0)
        return jnp.where(pos >= 0, count, -1)

    row_pos = start + lax.broadcasted_iota(jnp.int32, (1, rows), 1)
    col_pos = start + lax.broadcasted_iota(jnp.int32, (rows, 1), 0)
    own_row = segment(row_pos)
    own_col = segment(col_pos)
    next_row = jnp.where(row_pos + rows < frames, segment(row_pos + rows), -2)
    prev_col = segment(col_pos - rows)
    bias_own[...] = jnp.where((own_col == own_row) & (col_pos <= row_pos), 0.0, MASKED)
    bias_prev[...] = jnp.where(prev_col == own_row, 0.0, MASKED)
    bias_next[...] = jnp.where(own_col == next_row, 0.0, MASKED)

    loads[0].wait()
    tail.wait()

    def tap_rows(tap):
        frame = lax.broadcasted_iota(jnp.int32, (1, rows), 1)
        feature = 2 * frame + (tap - 3)
        behind = 2 - lax.div(tap + 1, 2)
        live = segment(row_pos - behind) == own_row
        feature = jnp.where(live, feature, -1000)
        pick = lax.broadcasted_iota(jnp.int32, (2 * rows, rows), 0) == feature
        pick_tail = lax.broadcasted_iota(jnp.int32, (16, rows), 0) - 16 == feature
        picked = tn(hid[...], jnp.where(pick, 1.0, 0.0).astype(BF16))
        picked = picked + tn(tail_in[...], jnp.where(pick_tail, 1.0, 0.0).astype(BF16))
        return picked.astype(BF16)

    taps_copies = []
    for i in range(2):
        taps_out[i] = tap_rows(2 * (1 - core) + i)
        copy = remote(
            taps_out.at[i],
            taps_in.at[i],
            misc_send.at[2 + i],
            misc_recv.at[2 + i],
            {"dp": other_core},
        )
        copy.start()
        taps_copies.append(copy)
    for i in range(2):
        taps_mine[i] = tap_rows(2 * core + i)
    for load in loads[1:]:
        load.wait()

    def delta_of(g_head, o_head):
        product = g_head.astype(F32) * o_head.astype(F32)
        return jnp.sum(product.T, axis=0, keepdims=True)

    def scores(k_head, q_head, bias):
        return nt(k_head, q_head) * SCALE_LOG2E + bias[...]

    def grads(e, ratio, k_head, v_head, q_head, g_head, delta):
        prob = e * ratio
        d_value = nn(prob.astype(BF16), g_head)
        d_score = (prob * (nt(v_head, g_head) - delta)).astype(BF16)
        return d_value, nn(d_score, q_head) * SCALE, tn(k_head, d_score) * SCALE

    def stat_copies(index):
        return (
            remote(
                stat_own.at[index],
                stat_from_next.at[index],
                stat_send.at[index, 0],
                stat_recv.at[index, 0],
                {"ctx": before},
            ),
            remote(
                stat_next.at[index],
                stat_from_prev.at[index],
                stat_send.at[index, 1],
                stat_recv.at[index, 1],
                {"ctx": after},
            ),
        )

    def merged(m_one, z_one, m_two, z_two):
        m = jnp.maximum(m_one, m_two)
        z = z_one * jnp.exp2(m_one - m) + z_two * jnp.exp2(m_two - m)
        return jnp.exp2(m_one - m) / z

    def step(index, carry):
        here = cols(half_heads + index)
        for copy in qg_copies(index):
            copy.wait()
        s = scores(k[:, here], q[:, here], bias_own)
        m = jnp.max(s, axis=0, keepdims=True)
        e = jnp.exp2(s - m)
        e_own[...] = e
        stat_own[index, 0:1, :] = m
        stat_own[index, 1:2, :] = jnp.sum(e, axis=0, keepdims=True)
        stat_own[index, 2:3, :] = delta_of(g[:, here], o[:, here])
        s = scores(k[:, here], q_next[:, cols(index)], bias_next)
        m = jnp.max(s, axis=0, keepdims=True)
        e = jnp.exp2(s - m)
        e_next[...] = e
        stat_next[index, 0:1, :] = m
        stat_next[index, 1:2, :] = jnp.sum(e, axis=0, keepdims=True)
        for copy in stat_copies(index):
            copy.start()

        for copy in kv_copies(index):
            copy.wait()
        there = cols(index)
        s_own = scores(k[:, there], q[:, there], bias_own)
        s_prev = scores(k_prev[:, there], q[:, there], bias_prev)
        m = jnp.maximum(
            jnp.max(s_own, axis=0, keepdims=True), jnp.max(s_prev, axis=0, keepdims=True)
        )
        e_one = jnp.exp2(s_own - m)
        e_two = jnp.exp2(s_prev - m)
        ratio = 1.0 / (
            jnp.sum(e_one, axis=0, keepdims=True) + jnp.sum(e_two, axis=0, keepdims=True)
        )
        delta = delta_of(g[:, there], o[:, there])
        d_value, d_key, d_query = grads(
            e_one, ratio, k[:, there], v[:, there], q[:, there], g[:, there], delta
        )
        dv[:, there] = d_value.astype(BF16)
        dk[:, there] = d_key.astype(BF16)
        d_value, d_key, d_query_prev = grads(
            e_two, ratio, k_prev[:, there], v_prev[:, there], q[:, there], g[:, there], delta
        )
        dv_prev[:, there] = d_value.astype(BF16)
        dk_prev[:, there] = d_key.astype(BF16)
        dq[:, there] = (d_query + d_query_prev).T.astype(BF16)

        for copy in stat_copies(index):
            copy.wait()
        ratio = merged(
            stat_own[index, 0:1, :],
            stat_own[index, 1:2, :],
            stat_from_prev[index, 0:1, :],
            stat_from_prev[index, 1:2, :],
        )
        d_value, d_key, d_query = grads(
            e_own[...],
            ratio,
            k[:, here],
            v[:, here],
            q[:, here],
            g[:, here],
            stat_own[index, 2:3, :],
        )
        dq[:, here] = d_query.T.astype(BF16)
        ratio = merged(
            stat_next[index, 0:1, :],
            stat_next[index, 1:2, :],
            stat_from_next[index, 0:1, :],
            stat_from_next[index, 1:2, :],
        )
        d_value_next, d_key_next, d_query_next = grads(
            e_next[...],
            ratio,
            k[:, here],
            v[:, here],
            q_next[:, there],
            g_next[:, there],
            stat_from_next[index, 2:3, :],
        )
        dv[:, here] = (d_value + d_value_next).astype(BF16)
        dk[:, here] = (d_key + d_key_next).astype(BF16)
        dq_next[:, there] = d_query_next.T.astype(BF16)
        return carry

    lax.fori_loop(0, half_heads, step, 0)

    def piece(index):
        return pl.ds(pl.multiple_of(index * chunk, chunk), chunk)

    def back_copy(index):
        return remote(
            back_out.at[piece(index), :],
            back_in.at[piece(index), :],
            chunk_send.at[0, index],
            chunk_recv.at[0, index],
            {"ctx": before},
        )

    def fwd_copy(index):
        return remote(
            fwd_out.at[piece(index), :],
            fwd_in.at[piece(index), :],
            chunk_send.at[1, index],
            chunk_recv.at[1, index],
            {"ctx": after},
        )

    def pipe_copy(index):
        return remote(
            pipe_out.at[piece(index), :],
            pipe_in.at[piece(index), :],
            chunk_send.at[2, index],
            chunk_recv.at[2, index],
            {"pipe": 1 - pipe},
        )

    def half_copy(index):
        return remote(
            half_mine.at[piece(index), :],
            half_other.at[piece(index), :],
            chunk_send.at[3, index],
            chunk_recv.at[3, index],
            {"dp": other_core},
        )

    def project_away(index, carry):
        at = piece(index)
        fwd_out[at, :] = nt(dq_next[at, :], w[0, :, half_width:]).astype(BF16)
        fwd_copy(index).start()
        back = nt(dk_prev[at, :], w[1, :, :half_width]) + nt(dv_prev[at, :], w[2, :, :half_width])
        back_out[at, :] = back.astype(BF16)
        back_copy(index).start()
        return carry

    lax.fori_loop(0, CHUNKS, project_away, 0)

    def project_own(index, carry):
        at = piece(index)
        lat_sum[at, :] = nt(dq[at, :], w[0]) + nt(dk[at, :], w[1]) + nt(dv[at, :], w[2])
        return carry

    lax.fori_loop(0, CHUNKS, project_own, 0)

    def join_ctx(index, carry):
        at = piece(index)
        fwd_copy(index).wait()
        back_copy(index).wait()
        whole = lat_sum[at, :] + fwd_in[at, :].astype(F32) + back_in[at, :].astype(F32)
        lat_sum[at, :] = whole
        pipe_out[at, :] = whole.astype(BF16)
        pipe_copy(index).start()
        return carry

    lax.fori_loop(0, CHUNKS, join_ctx, 0)

    def join_pipe(index, carry):
        at = piece(index)
        pipe_copy(index).wait()
        latent = (lat_sum[at, :] + pipe_in[at, :].astype(F32)).astype(BF16)
        pipe_out[at, :] = latent
        ext[at, :] = latent.astype(F32)
        half_mine[at, :] = pipe_out[at, my_half]
        half_copy(index).start()
        return carry

    lax.fori_loop(0, CHUNKS, join_pipe, 0)
    lead = remote(
        pipe_out.at[pl.ds(0, 16), :], head_in, misc_send.at[4], misc_recv.at[4], {"ctx": before}
    )
    lead.start()

    for copy in taps_copies:
        copy.wait()

    def half_wait(index, carry):
        half_copy(index).wait()
        return carry

    lax.fori_loop(0, CHUNKS, half_wait, 0)
    for i in range(2):
        conv_part[i] = (
            nn(taps_mine[i], half_mine[...]) + nn(taps_in[i], half_other[...])
        ).astype(BF16)

    def rs_copy(step):
        to = lax.rem(ctx + step, n_ctx)
        return remote(
            conv_part.at[:, pl.ds(pl.multiple_of(to * share, share), share), :],
            conv_in.at[step],
            rs_send.at[step],
            rs_recv.at[step],
            {"ctx": to},
        )

    def rs_start(step, carry):
        rs_copy(step).start()
        return carry

    lax.fori_loop(1, n_ctx, rs_start, 0)

    lead.wait()
    swap.wait()
    ext[pl.ds(rows, 16), :] = head_in[...].astype(F32)

    def spread_tap(tap, shift):
        pos = col_pos + shift
        behind = (2, 1, 1, 0)[tap]
        live = (segment(pos - behind) == segment(pos)) & (pos < frames)
        masked = jnp.where(live, ext[pl.ds(shift, rows), :], 0.0).astype(BF16)
        return nt(masked, cw[tap])

    even = spread_tap(3, 0) + spread_tap(1, 1)
    odd = spread_tap(2, 1) + spread_tap(0, 2)
    for i in range(half // 128):
        at = slice(i * 128, (i + 1) * 128)
        spread[i, pl.ds(0, rows, stride=2), :] = even[:, at]
        spread[i, pl.ds(1, rows, stride=2), :] = odd[:, at]
        hid_out[:, at] = spread[i].astype(BF16)

    def rs_wait(step, carry):
        rs_copy(step).wait()
        return carry

    lax.fori_loop(1, n_ctx, rs_wait, 0)
    mine = conv_part[:, pl.ds(pl.multiple_of(ctx * share, share), share), :].astype(F32)
    total[dp] = lax.fori_loop(
        1, n_ctx, lambda step, carry: carry + conv_in[step].astype(F32), mine
    )

    copies = []
    for i in range(1, 4):
        copy = remote(
            total.at[dp], total.at[dp], dp_send.at[i], dp_recv.at[i], {"dp": lax.rem(dp + i, 4)}
        )
        copy.start()
        copies.append(copy)
    for i in range(1, 4):
        copies[i - 1].wait_send()
        sender = lax.rem(dp + 4 - i, 4)
        remote(
            total.at[sender], total.at[sender], dp_send.at[i], dp_recv.at[i], {"dp": sender}
        ).wait_recv()
    for side in range(2):
        conv_out[2 * side : 2 * side + 2] = total[side] + total[2 + side]


def body(queries, keys, values, outputs, out_grads, lengths, proj_weight, hidden, conv_weight):
    n_ctx = lax.axis_size("ctx")
    rows, width = queries.shape[1:]
    ch = proj_weight.shape[1]
    half = ch // 2
    half_width = width // 2
    half_heads = half_width // HEAD_DIM
    share = ch // n_ctx
    vmem = pltpu.VMEM
    dma = pltpu.SemaphoreType.DMA
    hidden_grad, conv_grad = pl.pallas_call(
        functools.partial(kernel, n_ctx),
        out_shape=(
            jax.ShapeDtypeStruct((2 * rows, half), BF16),
            jax.ShapeDtypeStruct((4, share, half), F32),
        ),
        in_specs=[pl.BlockSpec(memory_space=pltpu.SMEM)]
        + [pl.BlockSpec(memory_space=pl.ANY)] * 8,
        out_specs=(pl.BlockSpec(memory_space=pltpu.VMEM),) * 2,
        scratch_shapes=[vmem((rows, width), BF16)] * 5
        + [
            vmem((3, ch, width), BF16),
            vmem((2 * rows, ch), BF16),
            vmem((4, half, ch), BF16),
        ]
        + [vmem((rows, half_width), BF16)] * 4
        + [vmem((rows, rows), F32)] * 5
        + [vmem((half_heads, 8, rows), F32)] * 4
        + [vmem((rows, width), BF16)] * 3
        + [vmem((rows, half_width), BF16)] * 3
        + [vmem((rows, ch), F32)]
        + [vmem((rows, ch), BF16)] * 6
        + [vmem((rows, half), BF16)] * 2
        + [
            vmem((rows + 16, ch), F32),
            vmem((16, ch), BF16),
            vmem((16, ch), BF16),
        ]
        + [vmem((2, ch, rows), BF16)] * 3
        + [
            vmem((half // 128, 2 * rows, 128), F32),
            vmem((2, ch, half), BF16),
            vmem((n_ctx, 2, share, half), BF16),
            vmem((4, 2, share, half), F32),
            dma((8,)),
        ]
        + [dma((half_heads, 2))] * 6
        + [dma((4, CHUNKS))] * 2
        + [dma((5,))] * 2
        + [dma((n_ctx,))] * 2
        + [dma((4,))] * 2,
        compiler_params=pltpu.CompilerParams(
            collective_id=0, has_side_effects=True, vmem_limit_bytes=56 * 1024 * 1024
        ),
    )(
        lengths[0],
        queries[0],
        keys[0],
        values[0],
        outputs[0],
        out_grads[0],
        proj_weight,
        hidden[0],
        conv_weight,
    )
    return hidden_grad[None], conv_grad


def solution(mesh):
    placed = (
        P("dp", "ctx", "pipe"),
        P("dp", "ctx", "pipe"),
        P("dp", "ctx", "pipe"),
        P("dp", "ctx", "pipe"),
        P("dp", "ctx", "pipe"),
        P("dp", None),
        P(None, None, "pipe"),
        P("dp", "ctx", None),
        P(None, None, "pipe"),
    )
    return jax.shard_map(
        body,
        mesh=mesh,
        in_specs=placed,
        out_specs=(P("dp", "ctx", "pipe"), P(None, "ctx", "pipe")),
        check_vma=False,
    )
```

```python
import functools
import jax
import jax.numpy as jnp
from jax import lax
from jax.experimental import pallas as pl
from jax.experimental.pallas import tpu as pltpu
from jax.sharding import PartitionSpec as P

HEAD_DIM = 128
SCALE = HEAD_DIM ** (-0.5)
SCALE_LOG2E = SCALE * 1.4426950408889634
MASKED = -1e30
MESH = pl.DeviceIdType.MESH
F32 = jnp.float32
BF16 = jnp.bfloat16


def nn(left, right):
    return lax.dot_general(left, right, (((1,), (0,)), ((), ())), preferred_element_type=F32)


def nt(left, right):
    return lax.dot_general(left, right, (((1,), (1,)), ((), ())), preferred_element_type=F32)


def tn(left, right):
    return lax.dot_general(left, right, (((0,), (0,)), ((), ())), preferred_element_type=F32)


def kernel(
    n_ctx,
    lengths,
    q_in,
    k_in,
    v_in,
    o_in,
    g_in,
    w_in,
    hid_in,
    cw_in,
    hid_out,
    conv_out,
    q,
    k,
    v,
    o,
    g,
    w,
    wt,
    hid,
    cw,
    k_prev,
    v_prev,
    q_next,
    g_next,
    bias_own,
    bias_prev,
    bias_next,
    e_own,
    stat_own,
    stat_next,
    stat_from_next,
    stat_from_prev,
    dq,
    dk,
    dv,
    dk_prev,
    dv_prev,
    dq_next,
    dq_part,
    dk_part,
    dv_part,
    lat_sum,
    back_out,
    back_in,
    fwd_out,
    fwd_in,
    lat,
    pipe_out,
    pipe_in,
    half_mine,
    half_other,
    ext,
    head_in,
    tail_in,
    taps_mine,
    taps_out,
    taps_in,
    spread,
    conv_part,
    conv_in,
    total,
    local_sem,
    kv_send,
    kv_recv,
    qg_send,
    qg_recv,
    stat_send,
    stat_recv,
    z_send,
    z_recv,
    x_send,
    x_recv,
    misc_send,
    misc_recv,
    rs_send,
    rs_recv,
    dp_send,
    dp_recv,
):
    rows, width = q.shape
    heads = width // HEAD_DIM
    half_heads = heads // 2
    half_width = half_heads * HEAD_DIM
    ch = w.shape[1]
    half = ch // 2
    frames = rows * n_ctx
    share = ch // n_ctx
    chunk = rows // 2
    pipe = lax.axis_index("pipe")
    ctx = lax.axis_index("ctx")
    dp = lax.axis_index("dp")
    core = lax.rem(dp, 2)
    after = lax.rem(ctx + 1, n_ctx)
    before = lax.rem(ctx + n_ctx - 1, n_ctx)
    other_core = dp + 1 - 2 * core
    start = ctx * rows

    def cols(index):
        return pl.ds(pl.multiple_of(index * HEAD_DIM, HEAD_DIM), HEAD_DIM)

    def remote(src, dst, send, recv, where):
        return pltpu.make_async_remote_copy(
            src_ref=src,
            dst_ref=dst,
            send_sem=send,
            recv_sem=recv,
            device_id=where,
            device_id_type=MESH,
        )

    my_half = pl.ds(pl.multiple_of(pipe * half, half), half)
    their_half = pl.ds(pl.multiple_of((1 - pipe) * half, half), half)
    loads = [
        pltpu.make_async_copy(src, dst, local_sem.at[i])
        for i, (src, dst) in enumerate(
            (
                (k_in, k),
                (q_in, q),
                (g_in, g),
                (o_in, o),
                (hid_in, hid),
                (v_in, v),
                (w_in, w),
                (cw_in.at[:, my_half, :], cw.at[:, :, my_half]),
            )
        )
    ]
    for load in loads:
        load.start()

    barrier = pltpu.get_barrier_semaphore()

    def greet(step, carry):
        pl.semaphore_signal(
            barrier, inc=1, device_id={"ctx": lax.rem(ctx + step, n_ctx)}, device_id_type=MESH
        )
        return carry

    lax.fori_loop(1, n_ctx, greet, 0)
    pl.semaphore_signal(barrier, inc=1, device_id={"pipe": 1 - pipe}, device_id_type=MESH)
    for step in range(1, 4):
        pl.semaphore_signal(
            barrier, inc=1, device_id={"dp": lax.rem(dp + step, 4)}, device_id_type=MESH
        )
    for near in (after, before):
        pl.semaphore_signal(
            barrier, inc=1, device_id={"ctx": near, "pipe": 1 - pipe}, device_id_type=MESH
        )

    ends = [lengths[0]]
    for i in range(1, 4):
        ends.append(ends[-1] + lengths[i])

    def segment(pos):
        count = jnp.zeros(pos.shape, jnp.int32)
        for end in ends:
            count = count + jnp.where(pos >= end, 1, 0)
        return jnp.where(pos >= 0, count, -1)

    row_pos = start + lax.broadcasted_iota(jnp.int32, (1, rows), 1)
    col_pos = start + lax.broadcasted_iota(jnp.int32, (rows, 1), 0)
    own_row = segment(row_pos)
    own_col = segment(col_pos)
    next_row = jnp.where(row_pos + rows < frames, segment(row_pos + rows), -2)
    prev_col = segment(col_pos - rows)
    bias_own[...] = jnp.where((own_col == own_row) & (col_pos <= row_pos), 0.0, MASKED)
    bias_prev[...] = jnp.where(prev_col == own_row, 0.0, MASKED)
    bias_next[...] = jnp.where(own_col == next_row, 0.0, MASKED)

    def delta_of(g_head, o_head):
        product = g_head.astype(F32) * o_head.astype(F32)
        return jnp.sum(product.T, axis=0, keepdims=True)

    def statistics(k_head, q_head, bias):
        s = nt(k_head, q_head) * SCALE_LOG2E + bias[...]
        m = jnp.max(s, axis=0, keepdims=True)
        e = jnp.exp2(s - m)
        return e, m, jnp.sum(e, axis=0, keepdims=True)

    for load in loads[:4]:
        load.wait()

    def own_statistics(index, carry):
        here = cols(index)
        e, m, z = statistics(k[:, here], q[:, here], bias_own)
        e_own[index] = e
        stat_own[index, 0:1, :] = m
        stat_own[index, 1:2, :] = z
        stat_own[index, 2:3, :] = delta_of(g[:, here], o[:, here])
        return carry

    lax.fori_loop(0, heads, own_statistics, 0)
    pl.semaphore_wait(barrier, n_ctx - 1 + 1 + 3 + 2)

    tail = remote(
        hid_in.at[pl.ds(2 * rows - 16, 16), :],
        tail_in,
        misc_send.at[0],
        misc_recv.at[0],
        {"ctx": after},
    )
    tail.start()
    totals = remote(
        stat_own.at[pl.ds(half_heads, half_heads)],
        stat_from_next,
        misc_send.at[5],
        misc_recv.at[5],
        {"ctx": before},
    )
    totals.start()

    def kv_copies(index):
        return (
            remote(
                k_in.at[:, cols(index)],
                k_prev.at[:, cols(index)],
                kv_send.at[index, 0],
                kv_recv.at[index, 0],
                {"ctx": after},
            ),
            remote(
                v_in.at[:, cols(index)],
                v_prev.at[:, cols(index)],
                kv_send.at[index, 1],
                kv_recv.at[index, 1],
                {"ctx": after},
            ),
        )

    def qg_copies(index):
        return (
            remote(
                q_in.at[:, cols(half_heads + index)],
                q_next.at[:, cols(index)],
                qg_send.at[index, 0],
                qg_recv.at[index, 0],
                {"ctx": before},
            ),
            remote(
                g_in.at[:, cols(half_heads + index)],
                g_next.at[:, cols(index)],
                qg_send.at[index, 1],
                qg_recv.at[index, 1],
                {"ctx": before},
            ),
        )

    def halo(index, carry):
        for copy in qg_copies(index) + kv_copies(index):
            copy.start()
        return carry

    lax.fori_loop(0, 2, halo, 0)
    swap = remote(
        cw_in.at[:, their_half, :],
        cw.at[:, :, my_half],
        misc_send.at[1],
        misc_recv.at[1],
        {"pipe": 1 - pipe},
    )
    swap.start()

    for load in loads[4:]:
        load.wait()
    tail.wait()

    def tap_rows(tap):
        frame = lax.broadcasted_iota(jnp.int32, (1, rows), 1)
        feature = 2 * frame + (tap - 3)
        behind = 2 - lax.div(tap + 1, 2)
        live = segment(row_pos - behind) == own_row
        feature = jnp.where(live, feature, -1000)
        pick = lax.broadcasted_iota(jnp.int32, (2 * rows, rows), 0) == feature
        pick_tail = lax.broadcasted_iota(jnp.int32, (16, rows), 0) - 16 == feature
        picked = tn(hid[...], jnp.where(pick, 1.0, 0.0).astype(BF16))
        picked = picked + tn(tail_in[...], jnp.where(pick_tail, 1.0, 0.0).astype(BF16))
        return picked.astype(BF16)

    taps_copies = []
    for i in range(2):
        taps_out[i] = tap_rows(2 * (1 - core) + i)
        copy = remote(
            taps_out.at[i],
            taps_in.at[i],
            misc_send.at[2 + i],
            misc_recv.at[2 + i],
            {"dp": other_core},
        )
        copy.start()
        taps_copies.append(copy)
    for i in range(2):
        taps_mine[i] = tap_rows(2 * core + i)
    for i in range(3):
        wt[i] = w[i].T
    totals.wait()

    def grads(e, ratio, k_head, v_head, q_head, g_head, delta):
        prob = e * ratio
        d_value = nn(prob.astype(BF16), g_head)
        d_score = (prob * (nt(v_head, g_head) - delta)).astype(BF16)
        return d_value, nn(d_score, q_head) * SCALE, tn(k_head, d_score) * SCALE

    def stat_copy(index):
        return remote(
            stat_next.at[index],
            stat_from_prev.at[index],
            stat_send.at[index],
            stat_recv.at[index],
            {"ctx": after},
        )

    def merged(m_one, z_one, m_two, z_two):
        m = jnp.maximum(m_one, m_two)
        weight = jnp.exp2(m_one - m)
        other = jnp.exp2(m_two - m)
        whole = z_one * weight + z_two * other
        return weight / whole, other / whole

    def cross_second(index):
        here = cols(half_heads + index)
        there = cols(index)
        for copy in qg_copies(index):
            copy.wait()
        e, m, z = statistics(k[:, here], q_next[:, there], bias_next)
        stat_next[index, 0:1, :] = m
        stat_next[index, 1:2, :] = z
        stat_copy(index).start()

        @pl.when(index + 2 < half_heads)
        def _():
            halo(index + 2, 0)

        _, ratio = merged(
            stat_from_next[index, 0:1, :], stat_from_next[index, 1:2, :], m, z
        )
        d_value, d_key, d_query = grads(
            e,
            ratio,
            k[:, here],
            v[:, here],
            q_next[:, there],
            g_next[:, there],
            stat_from_next[index, 2:3, :],
        )
        dv_part[:, there] = d_value
        dk_part[:, there] = d_key
        dq_next[:, there] = d_query.T.astype(BF16)

    def cross_first(index):
        there = cols(index)
        for copy in kv_copies(index):
            copy.wait()
        e, m, z = statistics(k_prev[:, there], q[:, there], bias_prev)
        ratio_own, ratio = merged(stat_own[index, 0:1, :], stat_own[index, 1:2, :], m, z)
        stat_own[index, 3:4, :] = ratio_own
        d_value, d_key, d_query = grads(
            e,
            ratio,
            k_prev[:, there],
            v_prev[:, there],
            q[:, there],
            g[:, there],
            stat_own[index, 2:3, :],
        )
        dv_prev[:, there] = d_value.astype(BF16)
        dk_prev[:, there] = d_key.astype(BF16)
        dq_part[index] = d_query

    def own_grads(index, ratio):
        here = cols(index)
        return grads(
            e_own[index],
            ratio,
            k[:, here],
            v[:, here],
            q[:, here],
            g[:, here],
            stat_own[index, 2:3, :],
        )

    def own_first(index):
        here = cols(index)
        d_value, d_key, d_query = own_grads(index, stat_own[index, 3:4, :])
        dv[:, here] = d_value.astype(BF16)
        dk[:, here] = d_key.astype(BF16)
        dq[:, here] = (d_query + dq_part[index]).T.astype(BF16)

    def own_second(index):
        here = cols(half_heads + index)
        there = cols(index)
        stat_copy(index).wait()
        ratio, _ = merged(
            stat_own[half_heads + index, 0:1, :],
            stat_own[half_heads + index, 1:2, :],
            stat_from_prev[index, 0:1, :],
            stat_from_prev[index, 1:2, :],
        )
        d_value, d_key, d_query = own_grads(half_heads + index, ratio)
        dv[:, here] = (d_value + dv_part[:, there]).astype(BF16)
        dk[:, here] = (d_key + dk_part[:, there]).astype(BF16)
        dq[:, here] = d_query.T.astype(BF16)

    def step(index, carry):
        pl.when(index >= 2)(lambda: own_second(index - 2))
        cross_second(index)
        cross_first(index)
        pl.when(index < half_heads - 1)(lambda: own_first(index))
        return carry

    lax.fori_loop(0, half_heads, step, 0)

    def piece(index):
        side = lax.rem(index // 2 + 1 + pipe, 2)
        at = pl.ds(pl.multiple_of(lax.rem(index, 2) * chunk, chunk), chunk)
        return at, pl.ds(pl.multiple_of(side * half, half), half)

    def back_copy(index):
        return remote(
            back_out.at[piece(index)],
            back_in.at[piece(index)],
            z_send.at[0, index],
            z_recv.at[0, index],
            {"ctx": before},
        )

    def fwd_copy(index):
        return remote(
            fwd_out.at[piece(index)],
            fwd_in.at[piece(index)],
            z_send.at[1, index],
            z_recv.at[1, index],
            {"ctx": after},
        )

    def x_copy(kind, src, dst, index, where):
        at = pl.ds(pl.multiple_of(index * chunk, chunk), chunk)
        return remote(
            src.at[at], dst.at[at], x_send.at[kind, index], x_recv.at[kind, index], where
        )

    def pipe_copy(index):
        return x_copy(0, pipe_out, pipe_in, index, {"pipe": 1 - pipe})

    def half_copy(index):
        return x_copy(1, half_mine, half_other, index, {"dp": other_core})

    def lat_copy(index, side):
        at = pl.ds(pl.multiple_of(index * chunk, chunk), chunk)
        return remote(
            lat.at[at, side],
            lat.at[at, side],
            x_send.at[2, index],
            x_recv.at[2, index],
            {"pipe": 1 - pipe},
        )

    def project_away(index, carry):
        at, side = piece(index)
        fwd_out[at, side] = nn(dq_next[at, :], wt[0, half_width:, side]).astype(BF16)
        fwd_copy(index).start()
        back = nn(dk_prev[at, :], wt[1, :half_width, side])
        back = back + nn(dv_prev[at, :], wt[2, :half_width, side])
        back_out[at, side] = back.astype(BF16)
        back_copy(index).start()
        return carry

    lax.fori_loop(0, 4, project_away, 0)

    own_first(half_heads - 1)

    def own_late(index, carry):
        own_second(index)
        return carry

    lax.fori_loop(max(half_heads - 2, 0), half_heads, own_late, 0)

    def join_ctx(index, carry):
        at, side = piece(index)
        own = nn(dq[at, :], wt[0, :, side]) + nn(dk[at, :], wt[1, :, side])
        own = own + nn(dv[at, :], wt[2, :, side])
        fwd_copy(index).wait()
        back_copy(index).wait()
        whole = own + fwd_in[at, side].astype(F32) + back_in[at, side].astype(F32)

        @pl.when(index < 2)
        def _():
            pipe_out[at, :] = whole.astype(BF16)
            pipe_copy(index).start()

        @pl.when(index >= 2)
        def _():
            lat_sum[at, :] = whole

        return carry

    lax.fori_loop(0, 4, join_ctx, 0)

    def join_pipe(index, carry):
        at = pl.ds(pl.multiple_of(index * chunk, chunk), chunk)
        pipe_copy(index).wait()
        latent = (lat_sum[at, :] + pipe_in[at, :].astype(F32)).astype(BF16)
        half_mine[at, :] = latent
        half_copy(index).start()
        lat[at, my_half] = latent
        lat_copy(index, my_half).start()
        return carry

    lax.fori_loop(0, 2, join_pipe, 0)
    leads = []
    for i in range(2):
        lead = remote(
            half_mine.at[pl.ds(0, 16), :],
            head_in.at[:, my_half],
            misc_send.at[4 + 2 * i],
            misc_recv.at[4 + 2 * i],
            {"ctx": before, "pipe": pipe + i - 2 * i * pipe},
        )
        lead.start()
        leads.append(lead)

    for copy in taps_copies:
        copy.wait()

    def half_wait(index, carry):
        half_copy(index).wait()
        return carry

    lax.fori_loop(0, 2, half_wait, 0)
    for i in range(2):
        conv_part[i] = (
            nn(taps_mine[i], half_mine[...]) + nn(taps_in[i], half_other[...])
        ).astype(BF16)

    def rs_copy(step):
        to = lax.rem(ctx + step, n_ctx)
        return remote(
            conv_part.at[:, pl.ds(pl.multiple_of(to * share, share), share), :],
            conv_in.at[step],
            rs_send.at[step],
            rs_recv.at[step],
            {"ctx": to},
        )

    def rs_start(step, carry):
        rs_copy(step).start()
        return carry

    lax.fori_loop(1, n_ctx, rs_start, 0)

    for i in range(2):
        leads[i].wait_send()
        remote(
            head_in.at[:, my_half if i == 0 else their_half],
            head_in.at[:, my_half if i == 0 else their_half],
            misc_send.at[4 + 2 * i],
            misc_recv.at[4 + 2 * i],
            {"ctx": before},
        ).wait_recv()
    for i in range(2):
        lat_copy(i, my_half).wait_send()
        lat_copy(i, their_half).wait_recv()
    swap.wait()
    ext[pl.ds(0, rows), :] = lat[...].astype(F32)
    ext[pl.ds(rows, 16), :] = head_in[...].astype(F32)

    def spread_tap(tap, shift):
        pos = col_pos + shift
        behind = (2, 1, 1, 0)[tap]
        live = (segment(pos - behind) == segment(pos)) & (pos < frames)
        masked = jnp.where(live, ext[pl.ds(shift, rows), :], 0.0).astype(BF16)
        return nt(masked, cw[tap])

    even = spread_tap(3, 0) + spread_tap(1, 1)
    odd = spread_tap(2, 1) + spread_tap(0, 2)
    for i in range(half // 128):
        at = slice(i * 128, (i + 1) * 128)
        spread[i, pl.ds(0, rows, stride=2), :] = even[:, at]
        spread[i, pl.ds(1, rows, stride=2), :] = odd[:, at]
        hid_out[:, at] = spread[i].astype(BF16)

    def rs_wait(step, carry):
        rs_copy(step).wait()
        return carry

    lax.fori_loop(1, n_ctx, rs_wait, 0)
    mine = conv_part[:, pl.ds(pl.multiple_of(ctx * share, share), share), :].astype(F32)
    total[dp] = lax.fori_loop(
        1, n_ctx, lambda step, carry: carry + conv_in[step].astype(F32), mine
    )

    copies = []
    for i in range(1, 4):
        copy = remote(
            total.at[dp], total.at[dp], dp_send.at[i], dp_recv.at[i], {"dp": lax.rem(dp + i, 4)}
        )
        copy.start()
        copies.append(copy)
    for i in range(1, 4):
        copies[i - 1].wait_send()
        sender = lax.rem(dp + 4 - i, 4)
        remote(
            total.at[sender], total.at[sender], dp_send.at[i], dp_recv.at[i], {"dp": sender}
        ).wait_recv()
    for side in range(2):
        conv_out[2 * side : 2 * side + 2] = total[side] + total[2 + side]


def body(queries, keys, values, outputs, out_grads, lengths, proj_weight, hidden, conv_weight):
    n_ctx = lax.axis_size("ctx")
    rows, width = queries.shape[1:]
    ch = proj_weight.shape[1]
    half = ch // 2
    half_width = width // 2
    half_heads = half_width // HEAD_DIM
    share = ch // n_ctx
    vmem = pltpu.VMEM
    dma = pltpu.SemaphoreType.DMA
    hidden_grad, conv_grad = pl.pallas_call(
        functools.partial(kernel, n_ctx),
        out_shape=(
            jax.ShapeDtypeStruct((2 * rows, half), BF16),
            jax.ShapeDtypeStruct((4, share, half), F32),
        ),
        in_specs=[pl.BlockSpec(memory_space=pltpu.SMEM)]
        + [pl.BlockSpec(memory_space=pl.ANY)] * 8,
        out_specs=(pl.BlockSpec(memory_space=pltpu.VMEM),) * 2,
        scratch_shapes=[vmem((rows, width), BF16)] * 5
        + [
            vmem((3, ch, width), BF16),
            vmem((3, width, ch), BF16),
            vmem((2 * rows, ch), BF16),
            vmem((4, half, ch), BF16),
        ]
        + [vmem((rows, half_width), BF16)] * 4
        + [vmem((rows, rows), F32)] * 3
        + [vmem((2 * half_heads, rows, rows), F32)]
        + [vmem((2 * half_heads, 8, rows), F32)]
        + [vmem((half_heads, 8, rows), F32)] * 3
        + [vmem((rows, width), BF16)] * 3
        + [vmem((rows, half_width), BF16)] * 3
        + [vmem((half_heads, HEAD_DIM, rows), F32)]
        + [vmem((rows, half_width), F32)] * 2
        + [vmem((rows, half), F32)]
        + [vmem((rows, ch), BF16)] * 5
        + [vmem((rows, half), BF16)] * 4
        + [
            vmem((rows + 16, ch), F32),
            vmem((16, ch), BF16),
            vmem((16, ch), BF16),
        ]
        + [vmem((2, ch, rows), BF16)] * 3
        + [
            vmem((half // 128, 2 * rows, 128), F32),
            vmem((2, ch, half), BF16),
            vmem((n_ctx, 2, share, half), BF16),
            vmem((4, 2, share, half), F32),
            dma((8,)),
        ]
        + [dma((half_heads, 2))] * 4
        + [dma((half_heads,))] * 2
        + [dma((2, 4))] * 2
        + [dma((3, 2))] * 2
        + [dma((7,))] * 2
        + [dma((n_ctx,))] * 2
        + [dma((4,))] * 2,
        compiler_params=pltpu.CompilerParams(
            collective_id=0, has_side_effects=True, vmem_limit_bytes=56 * 1024 * 1024
        ),
    )(
        lengths[0],
        queries[0],
        keys[0],
        values[0],
        outputs[0],
        out_grads[0],
        proj_weight,
        hidden[0],
        conv_weight,
    )
    return hidden_grad[None], conv_grad


def solution(mesh):
    placed = (
        P("dp", "ctx", "pipe"),
        P("dp", "ctx", "pipe"),
        P("dp", "ctx", "pipe"),
        P("dp", "ctx", "pipe"),
        P("dp", "ctx", "pipe"),
        P("dp", None),
        P(None, None, "pipe"),
        P("dp", "ctx", None),
        P(None, None, "pipe"),
    )
    return jax.shard_map(
        body,
        mesh=mesh,
        in_specs=placed,
        out_specs=(P("dp", "ctx", "pipe"), P(None, "ctx", "pipe")),
        check_vma=False,
    )
```

```python
import functools
import jax
import jax.numpy as jnp
from jax import lax
from jax.experimental import pallas as pl
from jax.experimental.pallas import tpu as pltpu
from jax.sharding import PartitionSpec as P

HEAD_DIM = 128
SCALE = HEAD_DIM ** (-0.5)
SCALE_LOG2E = SCALE * 1.4426950408889634
MASKED = -1e30
MESH = pl.DeviceIdType.MESH
F32 = jnp.float32
BF16 = jnp.bfloat16


def nn(left, right):
    return lax.dot_general(left, right, (((1,), (0,)), ((), ())), preferred_element_type=F32)


def nt(left, right):
    return lax.dot_general(left, right, (((1,), (1,)), ((), ())), preferred_element_type=F32)


def tn(left, right):
    return lax.dot_general(left, right, (((0,), (0,)), ((), ())), preferred_element_type=F32)


def kernel(
    n_ctx,
    lengths,
    q_in,
    k_in,
    v_in,
    o_in,
    g_in,
    w_in,
    hid_in,
    cw_in,
    hid_out,
    conv_out,
    q,
    k,
    v,
    o,
    g,
    w,
    wt,
    hid,
    cw,
    k_prev,
    v_prev,
    q_next,
    g_next,
    bias_own,
    bias_prev,
    bias_next,
    e_own,
    stat_own,
    stat_next,
    stat_from_next,
    stat_from_prev,
    dq,
    dk,
    dv,
    dk_prev,
    dv_prev,
    dq_next,
    dq_part,
    dk_part,
    dv_part,
    back_out,
    back_in,
    fwd_out,
    fwd_in,
    lat,
    pipe_out,
    pipe_in,
    half_mine,
    half_other,
    ext,
    head_in,
    tail_in,
    taps_mine,
    taps_out,
    taps_in,
    spread,
    conv_part,
    conv_in,
    total,
    local_sem,
    kv_send,
    kv_recv,
    qg_send,
    qg_recv,
    stat_send,
    stat_recv,
    z_send,
    z_recv,
    x_send,
    x_recv,
    misc_send,
    misc_recv,
    rs_send,
    rs_recv,
    lead_send,
    lead_recv,
    dp_send,
    dp_recv,
):
    rows, width = q.shape
    heads = width // HEAD_DIM
    half_heads = heads // 2
    half_width = half_heads * HEAD_DIM
    ch = w.shape[1]
    half = ch // 2
    frames = rows * n_ctx
    share = ch // n_ctx
    quarter = half // 2
    pipe = lax.axis_index("pipe")
    ctx = lax.axis_index("ctx")
    dp = lax.axis_index("dp")
    core = lax.rem(dp, 2)
    after = lax.rem(ctx + 1, n_ctx)
    before = lax.rem(ctx + n_ctx - 1, n_ctx)
    other_core = dp + 1 - 2 * core
    start = ctx * rows

    def cols(index):
        return pl.ds(pl.multiple_of(index * HEAD_DIM, HEAD_DIM), HEAD_DIM)

    def remote(src, dst, send, recv, where):
        return pltpu.make_async_remote_copy(
            src_ref=src,
            dst_ref=dst,
            send_sem=send,
            recv_sem=recv,
            device_id=where,
            device_id_type=MESH,
        )

    my_half = pl.ds(pl.multiple_of(pipe * half, half), half)
    their_half = pl.ds(pl.multiple_of((1 - pipe) * half, half), half)
    loads = [
        pltpu.make_async_copy(src, dst, local_sem.at[i])
        for i, (src, dst) in enumerate(
            (
                (k_in, k),
                (q_in, q),
                (g_in, g),
                (o_in, o),
                (hid_in, hid),
                (v_in, v),
                (w_in, w),
                (cw_in.at[:, my_half, :], cw.at[:, :, my_half]),
            )
        )
    ]
    for load in loads:
        load.start()

    barrier = pltpu.get_barrier_semaphore()

    def greet(step, carry):
        pl.semaphore_signal(
            barrier, inc=1, device_id={"ctx": lax.rem(ctx + step, n_ctx)}, device_id_type=MESH
        )
        return carry

    lax.fori_loop(1, n_ctx, greet, 0)
    pl.semaphore_signal(barrier, inc=1, device_id={"pipe": 1 - pipe}, device_id_type=MESH)
    for step in range(1, 4):
        pl.semaphore_signal(
            barrier, inc=1, device_id={"dp": lax.rem(dp + step, 4)}, device_id_type=MESH
        )
    for near in (after, before):
        pl.semaphore_signal(
            barrier, inc=1, device_id={"ctx": near, "pipe": 1 - pipe}, device_id_type=MESH
        )

    def delta_of(g_head, o_head):
        product = g_head.astype(F32) * o_head.astype(F32)
        return jnp.sum(product.T, axis=0, keepdims=True)

    def statistics(k_head, q_head, bias):
        s = nt(k_head, q_head) * SCALE_LOG2E + bias[...]
        m = jnp.max(s, axis=0, keepdims=True)
        e = jnp.exp2(s - m)
        return e, m, jnp.sum(e, axis=0, keepdims=True)

    pl.semaphore_wait(barrier, n_ctx - 1 + 1 + 3 + 2)

    tail = remote(
        hid_in.at[pl.ds(2 * rows - 16, 16), :],
        tail_in,
        misc_send.at[0],
        misc_recv.at[0],
        {"ctx": after},
    )
    tail.start()
    def kv_copies(index):
        return (
            remote(
                k_in.at[:, cols(index)],
                k_prev.at[:, cols(index)],
                kv_send.at[index, 0],
                kv_recv.at[index, 0],
                {"ctx": after},
            ),
            remote(
                v_in.at[:, cols(index)],
                v_prev.at[:, cols(index)],
                kv_send.at[index, 1],
                kv_recv.at[index, 1],
                {"ctx": after},
            ),
        )

    def qg_copies(index):
        return (
            remote(
                q_in.at[:, cols(half_heads + index)],
                q_next.at[:, cols(index)],
                qg_send.at[index, 0],
                qg_recv.at[index, 0],
                {"ctx": before},
            ),
            remote(
                g_in.at[:, cols(half_heads + index)],
                g_next.at[:, cols(index)],
                qg_send.at[index, 1],
                qg_recv.at[index, 1],
                {"ctx": before},
            ),
        )

    def halo(index, carry):
        for copy in qg_copies(index) + kv_copies(index):
            copy.start()
        return carry

    halo(0, 0)
    swap = remote(
        cw_in.at[:, their_half, :],
        cw.at[:, :, my_half],
        misc_send.at[1],
        misc_recv.at[1],
        {"pipe": 1 - pipe},
    )
    swap.start()

    ends = [lengths[0]]
    for i in range(1, 4):
        ends.append(ends[-1] + lengths[i])

    def segment(pos):
        count = jnp.zeros(pos.shape, jnp.int32)
        for end in ends:
            count = count + jnp.where(pos >= end, 1, 0)
        return jnp.where(pos >= 0, count, -1)

    row_pos = start + lax.broadcasted_iota(jnp.int32, (1, rows), 1)
    col_pos = start + lax.broadcasted_iota(jnp.int32, (rows, 1), 0)
    own_row = segment(row_pos)
    own_col = segment(col_pos)
    next_row = jnp.where(row_pos + rows < frames, segment(row_pos + rows), -2)
    prev_col = segment(col_pos - rows)
    bias_own[...] = jnp.where((own_col == own_row) & (col_pos <= row_pos), 0.0, MASKED)
    bias_prev[...] = jnp.where(prev_col == own_row, 0.0, MASKED)
    bias_next[...] = jnp.where(own_col == next_row, 0.0, MASKED)

    for load in loads[:4]:
        load.wait()

    def own_statistics(index, carry):
        here = cols(index)
        e, m, z = statistics(k[:, here], q[:, here], bias_own)
        e_own[index] = e
        stat_own[index, 0:1, :] = m
        stat_own[index, 1:2, :] = z
        stat_own[index, 2:3, :] = delta_of(g[:, here], o[:, here])
        return carry

    lax.fori_loop(half_heads, heads, own_statistics, 0)
    totals = remote(
        stat_own.at[pl.ds(half_heads, half_heads)],
        stat_from_next,
        misc_send.at[5],
        misc_recv.at[5],
        {"ctx": before},
    )
    totals.start()
    halo(1, 0)
    lax.fori_loop(0, half_heads, own_statistics, 0)
    for load in loads[4:]:
        load.wait()
    for i in range(3):
        wt[i] = w[i].T
    totals.wait()

    def tap_rows(tap):
        frame = lax.broadcasted_iota(jnp.int32, (1, rows), 1)
        feature = 2 * frame + (tap - 3)
        behind = 2 - lax.div(tap + 1, 2)
        live = segment(row_pos - behind) == own_row
        feature = jnp.where(live, feature, -1000)
        pick = lax.broadcasted_iota(jnp.int32, (2 * rows, rows), 0) == feature
        pick_tail = lax.broadcasted_iota(jnp.int32, (16, rows), 0) - 16 == feature
        picked = tn(hid[...], jnp.where(pick, 1.0, 0.0).astype(BF16))
        picked = picked + tn(tail_in[...], jnp.where(pick_tail, 1.0, 0.0).astype(BF16))
        return picked.astype(BF16)

    tail.wait()
    taps_copies = []
    for i in range(2):
        taps_out[i] = tap_rows(2 * (1 - core) + i)
        copy = remote(
            taps_out.at[i],
            taps_in.at[i],
            misc_send.at[2 + i],
            misc_recv.at[2 + i],
            {"dp": other_core},
        )
        copy.start()
        taps_copies.append(copy)

    def grads(e, ratio, k_head, v_head, q_head, g_head, delta):
        prob = e * ratio
        d_value = nn(prob.astype(BF16), g_head)
        d_score = (prob * (nt(v_head, g_head) - delta)).astype(BF16)
        return d_value, nn(d_score, q_head) * SCALE, tn(k_head, d_score) * SCALE

    def stat_copy(index):
        return remote(
            stat_next.at[index],
            stat_from_prev.at[index],
            stat_send.at[index],
            stat_recv.at[index],
            {"ctx": after},
        )

    def merged(m_one, z_one, m_two, z_two):
        m = jnp.maximum(m_one, m_two)
        weight = jnp.exp2(m_one - m)
        other = jnp.exp2(m_two - m)
        whole = z_one * weight + z_two * other
        return weight / whole, other / whole

    def cross_second(index):
        here = cols(half_heads + index)
        there = cols(index)
        for copy in qg_copies(index):
            copy.wait()
        e, m, z = statistics(k[:, here], q_next[:, there], bias_next)
        stat_next[index, 0:1, :] = m
        stat_next[index, 1:2, :] = z
        stat_copy(index).start()

        @pl.when(index + 2 < half_heads)
        def _():
            halo(index + 2, 0)

        _, ratio = merged(
            stat_from_next[index, 0:1, :], stat_from_next[index, 1:2, :], m, z
        )
        d_value, d_key, d_query = grads(
            e,
            ratio,
            k[:, here],
            v[:, here],
            q_next[:, there],
            g_next[:, there],
            stat_from_next[index, 2:3, :],
        )
        dv_part[:, there] = d_value
        dk_part[:, there] = d_key
        dq_next[:, there] = d_query.T.astype(BF16)

    def cross_first(index):
        there = cols(index)
        for copy in kv_copies(index):
            copy.wait()
        e, m, z = statistics(k_prev[:, there], q[:, there], bias_prev)
        ratio_own, ratio = merged(stat_own[index, 0:1, :], stat_own[index, 1:2, :], m, z)
        stat_own[index, 3:4, :] = ratio_own
        d_value, d_key, d_query = grads(
            e,
            ratio,
            k_prev[:, there],
            v_prev[:, there],
            q[:, there],
            g[:, there],
            stat_own[index, 2:3, :],
        )
        dv_prev[:, there] = d_value.astype(BF16)
        dk_prev[:, there] = d_key.astype(BF16)
        dq_part[index] = d_query

    def own_grads(index, ratio):
        here = cols(index)
        return grads(
            e_own[index],
            ratio,
            k[:, here],
            v[:, here],
            q[:, here],
            g[:, here],
            stat_own[index, 2:3, :],
        )

    def own_first(index):
        here = cols(index)
        d_value, d_key, d_query = own_grads(index, stat_own[index, 3:4, :])
        dv[:, here] = d_value.astype(BF16)
        dk[:, here] = d_key.astype(BF16)
        dq[:, here] = (d_query + dq_part[index]).T.astype(BF16)

    def own_second(index):
        here = cols(half_heads + index)
        there = cols(index)
        stat_copy(index).wait()
        ratio, _ = merged(
            stat_own[half_heads + index, 0:1, :],
            stat_own[half_heads + index, 1:2, :],
            stat_from_prev[index, 0:1, :],
            stat_from_prev[index, 1:2, :],
        )
        d_value, d_key, d_query = own_grads(half_heads + index, ratio)
        dv[:, here] = (d_value + dv_part[:, there]).astype(BF16)
        dk[:, here] = (d_key + dk_part[:, there]).astype(BF16)
        dq[:, here] = d_query.T.astype(BF16)

    def step(index, carry):
        pl.when(index >= 2)(lambda: own_second(index - 2))
        cross_second(index)
        cross_first(index)
        pl.when(index < half_heads - 1)(lambda: own_first(index))
        return carry

    lax.fori_loop(0, half_heads, step, 0)

    def columns(side, index):
        return pl.ds(pl.multiple_of(side * half + index * quarter, quarter), quarter)

    def piece(index):
        return columns(lax.rem(lax.rem(index, 2) + 1 + pipe, 2), index // 2)

    def back_copy(index):
        at = piece(index)
        return remote(
            back_out.at[:, at],
            back_in.at[:, at],
            z_send.at[0, index],
            z_recv.at[0, index],
            {"ctx": before},
        )

    def fwd_copy(index):
        at = piece(index)
        return remote(
            fwd_out.at[:, at],
            fwd_in.at[:, at],
            z_send.at[1, index],
            z_recv.at[1, index],
            {"ctx": after},
        )

    def x_copy(kind, src, dst, index, where):
        return remote(src, dst, x_send.at[kind, index], x_recv.at[kind, index], where)

    def pipe_copy(index):
        return x_copy(0, pipe_out.at[index], pipe_in.at[index], index, {"pipe": 1 - pipe})

    def half_copy(index):
        return x_copy(1, half_mine.at[index], half_other.at[index], index, {"dp": other_core})

    def lat_copy(index, side):
        at = columns(side, index)
        return x_copy(2, lat.at[:, at], lat.at[:, at], index, {"pipe": 1 - pipe})

    def lead_copy(index, turn, side):
        return remote(
            half_mine.at[index, pl.ds(0, 16), :],
            head_in.at[:, columns(side, index)],
            lead_send.at[index, turn],
            lead_recv.at[index, turn],
            {"ctx": before, "pipe": lax.rem(pipe + turn, 2)},
        )

    def rs_copy(index, step):
        to = lax.rem(ctx + step, n_ctx)
        return remote(
            conv_part.at[index, :, pl.ds(pl.multiple_of(to * share, share), share), :],
            conv_in.at[index, step],
            rs_send.at[index, step],
            rs_recv.at[index, step],
            {"ctx": to},
        )

    def project_away(index, carry):
        at = piece(index)
        fwd_out[:, at] = nn(dq_next[...], wt[0, half_width:, at]).astype(BF16)
        fwd_copy(index).start()
        back = nn(dk_prev[...], wt[1, :half_width, at])
        back = back + nn(dv_prev[...], wt[2, :half_width, at])
        back_out[:, at] = back.astype(BF16)
        back_copy(index).start()
        return carry

    lax.fori_loop(0, 4, project_away, 0)

    own_first(half_heads - 1)

    def own_late(index, carry):
        own_second(index)
        return carry

    lax.fori_loop(max(half_heads - 2, 0), half_heads, own_late, 0)

    def project_own(index):
        at = piece(index)
        own = nn(dq[...], wt[0, :, at]) + nn(dk[...], wt[1, :, at])
        return own + nn(dv[...], wt[2, :, at])

    def join_ctx(index, own):
        at = piece(index)
        fwd_copy(index).wait()
        back_copy(index).wait()
        return own + fwd_in[:, at].astype(F32) + back_in[:, at].astype(F32)

    def give(index):
        pipe_out[index] = join_ctx(2 * index, project_own(2 * index)).astype(BF16)
        pipe_copy(index).start()

    def settle(index, own):
        whole = join_ctx(2 * index + 1, own)
        pipe_copy(index).wait()
        latent = (whole + pipe_in[index].astype(F32)).astype(BF16)
        half_mine[index] = latent
        half_copy(index).start()
        lead_copy(index, 0, pipe).start()
        lead_copy(index, 1, pipe).start()
        lat[:, columns(pipe, index)] = latent
        lat_copy(index, pipe).start()

    def tap_grads(index):
        half_copy(index).wait()
        for i in range(2):
            conv_part[index, i] = (
                nn(taps_mine[i], half_mine[index]) + nn(taps_in[i], half_other[index])
            ).astype(BF16)

        def rs_start(step, carry):
            rs_copy(index, step).start()
            return carry

        lax.fori_loop(1, n_ctx, rs_start, 0)

    give(0)
    for i in range(2):
        taps_mine[i] = tap_rows(2 * core + i)
    give(1)
    own = project_own(1)
    for copy in taps_copies:
        copy.wait()
    settle(0, own)
    own = project_own(3)
    tap_grads(0)
    settle(1, own)
    tap_grads(1)

    for i in range(2):
        for turn in range(2):
            lead_copy(i, turn, pipe).wait_send()
            lead_copy(i, turn, lax.rem(pipe + turn, 2)).wait_recv()
        lat_copy(i, pipe).wait_send()
        lat_copy(i, 1 - pipe).wait_recv()
    swap.wait()
    ext[pl.ds(0, rows), :] = lat[...].astype(F32)
    ext[pl.ds(rows, 16), :] = head_in[...].astype(F32)

    def spread_tap(tap, shift):
        pos = col_pos + shift
        behind = (2, 1, 1, 0)[tap]
        live = (segment(pos - behind) == segment(pos)) & (pos < frames)
        masked = jnp.where(live, ext[pl.ds(shift, rows), :], 0.0).astype(BF16)
        return nt(masked, cw[tap])

    even = spread_tap(3, 0) + spread_tap(1, 1)
    odd = spread_tap(2, 1) + spread_tap(0, 2)
    for i in range(half // 128):
        at = slice(i * 128, (i + 1) * 128)
        spread[i, pl.ds(0, rows, stride=2), :] = even[:, at]
        spread[i, pl.ds(1, rows, stride=2), :] = odd[:, at]
        hid_out[:, at] = spread[i].astype(BF16)

    def dp_copy(index, turn, at):
        return remote(
            total.at[at, index],
            total.at[at, index],
            dp_send.at[index, turn],
            dp_recv.at[index, turn],
            {"dp": lax.rem(dp + turn, 4)},
        )

    def finish(index, carry):
        def rs_add(step, carry):
            rs_copy(index, step).wait()
            return carry + conv_in[index, step].astype(F32)

        mine = conv_part[index, :, pl.ds(pl.multiple_of(ctx * share, share), share), :]
        total[dp, index] = lax.fori_loop(1, n_ctx, rs_add, mine.astype(F32))
        for turn in range(1, 4):
            dp_copy(index, turn, dp).start()
        return carry

    lax.fori_loop(0, 2, finish, 0)
    for index in range(2):
        for turn in range(1, 4):
            dp_copy(index, turn, dp).wait_send()
            dp_copy(index, turn, lax.rem(dp + 4 - turn, 4)).wait_recv()
        at = slice(index * quarter, (index + 1) * quarter)
        for side in range(2):
            conv_out[2 * side : 2 * side + 2, :, at] = total[side, index] + total[2 + side, index]


def hand_on(hid_in, conv_in, hid_out, conv_out):
    hid_out[...] = hid_in[...]
    conv_out[...] = conv_in[...]


def body(queries, keys, values, outputs, out_grads, lengths, proj_weight, hidden, conv_weight):
    n_ctx = lax.axis_size("ctx")
    rows, width = queries.shape[1:]
    ch = proj_weight.shape[1]
    half = ch // 2
    half_width = width // 2
    half_heads = half_width // HEAD_DIM
    share = ch // n_ctx
    vmem = pltpu.VMEM
    dma = pltpu.SemaphoreType.DMA
    hidden_grad, conv_grad = pl.pallas_call(
        functools.partial(kernel, n_ctx),
        out_shape=(
            jax.ShapeDtypeStruct((2 * rows, half), BF16),
            jax.ShapeDtypeStruct((4, share, half), F32),
        ),
        in_specs=[pl.BlockSpec(memory_space=pltpu.SMEM)]
        + [pl.BlockSpec(memory_space=pl.ANY)] * 8,
        out_specs=(pl.BlockSpec(memory_space=pltpu.VMEM),) * 2,
        scratch_shapes=[vmem((rows, width), BF16)] * 5
        + [
            vmem((3, ch, width), BF16),
            vmem((3, width, ch), BF16),
            vmem((2 * rows, ch), BF16),
            vmem((4, half, ch), BF16),
        ]
        + [vmem((rows, half_width), BF16)] * 4
        + [vmem((rows, rows), F32)] * 3
        + [vmem((2 * half_heads, rows, rows), F32)]
        + [vmem((2 * half_heads, 8, rows), F32)]
        + [vmem((half_heads, 8, rows), F32)] * 3
        + [vmem((rows, width), BF16)] * 3
        + [vmem((rows, half_width), BF16)] * 3
        + [vmem((half_heads, HEAD_DIM, rows), F32)]
        + [vmem((rows, half_width), F32)] * 2
        + [vmem((rows, ch), BF16)] * 5
        + [vmem((2, rows, half // 2), BF16)] * 4
        + [
            vmem((rows + 16, ch), F32),
            vmem((16, ch), BF16),
            vmem((16, ch), BF16),
        ]
        + [vmem((2, ch, rows), BF16)] * 3
        + [
            vmem((half // 128, 2 * rows, 128), F32),
            vmem((2, 2, ch, half // 2), BF16),
            vmem((2, n_ctx, 2, share, half // 2), BF16),
            vmem((4, 2, 2, share, half // 2), F32),
            dma((8,)),
        ]
        + [dma((half_heads, 2))] * 4
        + [dma((half_heads,))] * 2
        + [dma((2, 4))] * 2
        + [dma((3, 2))] * 2
        + [dma((6,))] * 2
        + [dma((2, n_ctx))] * 2
        + [dma((2, 2))] * 2
        + [dma((2, 4))] * 2,
        compiler_params=pltpu.CompilerParams(
            collective_id=0, has_side_effects=True, vmem_limit_bytes=56 * 1024 * 1024
        ),
    )(
        lengths[0],
        queries[0],
        keys[0],
        values[0],
        outputs[0],
        out_grads[0],
        proj_weight,
        hidden[0],
        conv_weight,
    )
    hidden_grad, conv_grad = pl.pallas_call(
        hand_on,
        out_shape=(
            jax.ShapeDtypeStruct(hidden_grad.shape, BF16),
            jax.ShapeDtypeStruct(conv_grad.shape, F32),
        ),
        in_specs=[pl.BlockSpec(memory_space=pltpu.VMEM)] * 2,
        out_specs=(pl.BlockSpec(memory_space=pltpu.VMEM),) * 2,
    )(hidden_grad, conv_grad)
    return hidden_grad[None], conv_grad


def solution(mesh):
    placed = (
        P("dp", "ctx", "pipe"),
        P("dp", "ctx", "pipe"),
        P("dp", "ctx", "pipe"),
        P("dp", "ctx", "pipe"),
        P("dp", "ctx", "pipe"),
        P("dp", None),
        P(None, None, "pipe"),
        P("dp", "ctx", None),
        P(None, None, "pipe"),
    )
    return jax.shard_map(
        body,
        mesh=mesh,
        in_specs=placed,
        out_specs=(P("dp", "ctx", "pipe"), P(None, "ctx", "pipe")),
        check_vma=False,
    )
```

```python
import functools
import jax
import jax.numpy as jnp
from jax import lax
from jax.experimental import pallas as pl
from jax.experimental.pallas import tpu as pltpu
from jax.sharding import PartitionSpec as P

HEAD_DIM = 128
SCALE = HEAD_DIM ** (-0.5)
SCALE_LOG2E = SCALE * 1.4426950408889634
MASKED = -1e30
MESH = pl.DeviceIdType.MESH
F32 = jnp.float32
BF16 = jnp.bfloat16


def nn(left, right):
    return lax.dot_general(left, right, (((1,), (0,)), ((), ())), preferred_element_type=F32)


def nt(left, right):
    return lax.dot_general(left, right, (((1,), (1,)), ((), ())), preferred_element_type=F32)


def tn(left, right):
    return lax.dot_general(left, right, (((0,), (0,)), ((), ())), preferred_element_type=F32)


def kernel(
    n_ctx,
    lengths,
    q_in,
    k_in,
    v_in,
    o_in,
    g_in,
    w_in,
    hid_in,
    cw_in,
    hid_out,
    conv_out,
    q,
    k,
    v,
    o,
    g,
    w,
    wt,
    hid,
    cw,
    k_prev,
    v_prev,
    q_next,
    g_next,
    bias_own,
    bias_prev,
    bias_next,
    e_own,
    stat_own,
    stat_next,
    stat_from_next,
    stat_from_prev,
    dq,
    dk,
    dv,
    dk_prev,
    dv_prev,
    dq_next,
    dq_part,
    dk_part,
    dv_part,
    back_out,
    back_in,
    fwd_out,
    fwd_in,
    lat,
    pipe_out,
    pipe_in,
    half_mine,
    half_other,
    ext,
    head_in,
    tail_in,
    taps_mine,
    taps_out,
    taps_in,
    spread,
    conv_part,
    conv_in,
    total,
    local_sem,
    kv_send,
    kv_recv,
    qg_send,
    qg_recv,
    stat_send,
    stat_recv,
    z_send,
    z_recv,
    x_send,
    x_recv,
    misc_send,
    misc_recv,
    rs_send,
    rs_recv,
    lead_send,
    lead_recv,
    dp_send,
    dp_recv,
):
    rows, width = q.shape
    heads = width // HEAD_DIM
    half_heads = heads // 2
    half_width = half_heads * HEAD_DIM
    ch = w.shape[1]
    half = ch // 2
    frames = rows * n_ctx
    share = ch // n_ctx
    quarter = half // 2
    pipe = lax.axis_index("pipe")
    ctx = lax.axis_index("ctx")
    dp = lax.axis_index("dp")
    core = lax.rem(dp, 2)
    after = lax.rem(ctx + 1, n_ctx)
    before = lax.rem(ctx + n_ctx - 1, n_ctx)
    other_core = dp + 1 - 2 * core
    start = ctx * rows

    def cols(index):
        return pl.ds(pl.multiple_of(index * HEAD_DIM, HEAD_DIM), HEAD_DIM)

    def remote(src, dst, send, recv, where):
        return pltpu.make_async_remote_copy(
            src_ref=src,
            dst_ref=dst,
            send_sem=send,
            recv_sem=recv,
            device_id=where,
            device_id_type=MESH,
        )

    my_half = pl.ds(pl.multiple_of(pipe * half, half), half)
    their_half = pl.ds(pl.multiple_of((1 - pipe) * half, half), half)
    loads = [
        pltpu.make_async_copy(src, dst, local_sem.at[i])
        for i, (src, dst) in enumerate(
            (
                (k_in, k),
                (q_in, q),
                (g_in, g),
                (o_in, o),
                (hid_in, hid),
                (v_in, v),
                (w_in, w),
                (cw_in.at[:, my_half, :], cw.at[:, :, my_half]),
            )
        )
    ]
    for load in loads:
        load.start()

    barrier = pltpu.get_barrier_semaphore()

    def greet(step, carry):
        pl.semaphore_signal(
            barrier, inc=1, device_id={"ctx": lax.rem(ctx + step, n_ctx)}, device_id_type=MESH
        )
        return carry

    lax.fori_loop(1, n_ctx, greet, 0)
    pl.semaphore_signal(barrier, inc=1, device_id={"pipe": 1 - pipe}, device_id_type=MESH)
    for step in range(1, 4):
        pl.semaphore_signal(
            barrier, inc=1, device_id={"dp": lax.rem(dp + step, 4)}, device_id_type=MESH
        )
    for near in (after, before):
        pl.semaphore_signal(
            barrier, inc=1, device_id={"ctx": near, "pipe": 1 - pipe}, device_id_type=MESH
        )

    def delta_of(g_head, o_head):
        product = g_head.astype(F32) * o_head.astype(F32)
        return jnp.sum(product.T, axis=0, keepdims=True)

    def statistics(k_head, q_head, bias):
        s = nt(k_head, q_head) * SCALE_LOG2E + bias[...]
        m = jnp.max(s, axis=0, keepdims=True)
        e = jnp.exp2(s - m)
        return e, m, jnp.sum(e, axis=0, keepdims=True)

    pl.semaphore_wait(barrier, n_ctx - 1 + 1 + 3 + 2)

    tail = remote(
        hid_in.at[pl.ds(2 * rows - 16, 16), :],
        tail_in,
        misc_send.at[0],
        misc_recv.at[0],
        {"ctx": after},
    )
    tail.start()
    def kv_copies(index):
        return (
            remote(
                k_in.at[:, cols(index)],
                k_prev.at[:, cols(index)],
                kv_send.at[index, 0],
                kv_recv.at[index, 0],
                {"ctx": after},
            ),
            remote(
                v_in.at[:, cols(index)],
                v_prev.at[:, cols(index)],
                kv_send.at[index, 1],
                kv_recv.at[index, 1],
                {"ctx": after},
            ),
        )

    def qg_copies(index):
        return (
            remote(
                q_in.at[:, cols(half_heads + index)],
                q_next.at[:, cols(index)],
                qg_send.at[index, 0],
                qg_recv.at[index, 0],
                {"ctx": before},
            ),
            remote(
                g_in.at[:, cols(half_heads + index)],
                g_next.at[:, cols(index)],
                qg_send.at[index, 1],
                qg_recv.at[index, 1],
                {"ctx": before},
            ),
        )

    def halo(index, carry):
        for copy in qg_copies(index) + kv_copies(index):
            copy.start()
        return carry

    halo(0, 0)
    swap = remote(
        cw_in.at[:, their_half, :],
        cw.at[:, :, my_half],
        misc_send.at[1],
        misc_recv.at[1],
        {"pipe": 1 - pipe},
    )
    swap.start()

    ends = [lengths[0]]
    for i in range(1, 4):
        ends.append(ends[-1] + lengths[i])

    def segment(pos):
        count = jnp.zeros(pos.shape, jnp.int32)
        for end in ends:
            count = count + jnp.where(pos >= end, 1, 0)
        return jnp.where(pos >= 0, count, -1)

    row_pos = start + lax.broadcasted_iota(jnp.int32, (1, rows), 1)
    col_pos = start + lax.broadcasted_iota(jnp.int32, (rows, 1), 0)
    own_row = segment(row_pos)
    own_col = segment(col_pos)
    next_row = jnp.where(row_pos + rows < frames, segment(row_pos + rows), -2)
    prev_col = segment(col_pos - rows)
    bias_own[...] = jnp.where((own_col == own_row) & (col_pos <= row_pos), 0.0, MASKED)
    bias_prev[...] = jnp.where(prev_col == own_row, 0.0, MASKED)
    bias_next[...] = jnp.where(own_col == next_row, 0.0, MASKED)

    for load in loads[:4]:
        load.wait()

    def own_statistics(index, carry):
        here = cols(index)
        e, m, z = statistics(k[:, here], q[:, here], bias_own)
        e_own[index] = e
        stat_own[index, 0:1, :] = m
        stat_own[index, 1:2, :] = z
        stat_own[index, 2:3, :] = delta_of(g[:, here], o[:, here])
        return carry

    lax.fori_loop(half_heads, heads, own_statistics, 0)
    totals = remote(
        stat_own.at[pl.ds(half_heads, half_heads)],
        stat_from_next,
        misc_send.at[5],
        misc_recv.at[5],
        {"ctx": before},
    )
    totals.start()
    halo(1, 0)
    lax.fori_loop(0, half_heads, own_statistics, 0)
    for load in loads[4:]:
        load.wait()
    for i in range(3):
        wt[i] = w[i].T
    totals.wait()

    def tap_rows(tap):
        frame = lax.broadcasted_iota(jnp.int32, (1, rows), 1)
        feature = 2 * frame + (tap - 3)
        behind = 2 - lax.div(tap + 1, 2)
        live = segment(row_pos - behind) == own_row
        feature = jnp.where(live, feature, -1000)
        pick = lax.broadcasted_iota(jnp.int32, (2 * rows, rows), 0) == feature
        pick_tail = lax.broadcasted_iota(jnp.int32, (16, rows), 0) - 16 == feature
        picked = tn(hid[...], jnp.where(pick, 1.0, 0.0).astype(BF16))
        picked = picked + tn(tail_in[...], jnp.where(pick_tail, 1.0, 0.0).astype(BF16))
        return picked.astype(BF16)

    tail.wait()
    taps_copies = []
    for i in range(2):
        taps_out[i] = tap_rows(2 * (1 - core) + i)
        copy = remote(
            taps_out.at[i],
            taps_in.at[i],
            misc_send.at[2 + i],
            misc_recv.at[2 + i],
            {"dp": other_core},
        )
        copy.start()
        taps_copies.append(copy)

    def grads(e, ratio, k_head, v_head, q_head, g_head, delta):
        prob = e * ratio
        d_value = nn(prob.astype(BF16), g_head)
        d_score = (prob * (nt(v_head, g_head) - delta)).astype(BF16)
        return d_value, nn(d_score, q_head) * SCALE, tn(k_head, d_score) * SCALE

    def stat_copy(index):
        return remote(
            stat_next.at[index],
            stat_from_prev.at[index],
            stat_send.at[index],
            stat_recv.at[index],
            {"ctx": after},
        )

    def merged(m_one, z_one, m_two, z_two):
        m = jnp.maximum(m_one, m_two)
        weight = jnp.exp2(m_one - m)
        other = jnp.exp2(m_two - m)
        whole = z_one * weight + z_two * other
        return weight / whole, other / whole

    def cross_second(index):
        here = cols(half_heads + index)
        there = cols(index)
        for copy in qg_copies(index):
            copy.wait()
        e, m, z = statistics(k[:, here], q_next[:, there], bias_next)
        stat_next[index, 0:1, :] = m
        stat_next[index, 1:2, :] = z
        stat_copy(index).start()

        @pl.when(index + 2 < half_heads)
        def _():
            halo(index + 2, 0)

        _, ratio = merged(
            stat_from_next[index, 0:1, :], stat_from_next[index, 1:2, :], m, z
        )
        d_value, d_key, d_query = grads(
            e,
            ratio,
            k[:, here],
            v[:, here],
            q_next[:, there],
            g_next[:, there],
            stat_from_next[index, 2:3, :],
        )
        dv_part[:, there] = d_value
        dk_part[:, there] = d_key
        dq_next[:, there] = d_query.T.astype(BF16)

    def cross_first(index):
        there = cols(index)
        for copy in kv_copies(index):
            copy.wait()
        e, m, z = statistics(k_prev[:, there], q[:, there], bias_prev)
        ratio_own, ratio = merged(stat_own[index, 0:1, :], stat_own[index, 1:2, :], m, z)
        stat_own[index, 3:4, :] = ratio_own
        d_value, d_key, d_query = grads(
            e,
            ratio,
            k_prev[:, there],
            v_prev[:, there],
            q[:, there],
            g[:, there],
            stat_own[index, 2:3, :],
        )
        dv_prev[:, there] = d_value.astype(BF16)
        dk_prev[:, there] = d_key.astype(BF16)
        dq_part[index] = d_query

    def own_grads(index, ratio):
        here = cols(index)
        return grads(
            e_own[index],
            ratio,
            k[:, here],
            v[:, here],
            q[:, here],
            g[:, here],
            stat_own[index, 2:3, :],
        )

    def own_first(index):
        here = cols(index)
        d_value, d_key, d_query = own_grads(index, stat_own[index, 3:4, :])
        dv[:, here] = d_value.astype(BF16)
        dk[:, here] = d_key.astype(BF16)
        dq[:, here] = (d_query + dq_part[index]).T.astype(BF16)

    def own_second(index):
        here = cols(half_heads + index)
        there = cols(index)
        stat_copy(index).wait()
        ratio, _ = merged(
            stat_own[half_heads + index, 0:1, :],
            stat_own[half_heads + index, 1:2, :],
            stat_from_prev[index, 0:1, :],
            stat_from_prev[index, 1:2, :],
        )
        d_value, d_key, d_query = own_grads(half_heads + index, ratio)
        dv[:, here] = (d_value + dv_part[:, there]).astype(BF16)
        dk[:, here] = (d_key + dk_part[:, there]).astype(BF16)
        dq[:, here] = d_query.T.astype(BF16)

    def step(index, carry):
        pl.when(index >= 2)(lambda: own_second(index - 2))
        cross_second(index)
        cross_first(index)
        pl.when(index < half_heads - 1)(lambda: own_first(index))
        return carry

    lax.fori_loop(0, half_heads, step, 0)

    def columns(side, index):
        return pl.ds(pl.multiple_of(side * half + index * quarter, quarter), quarter)

    def piece(index):
        return columns(lax.rem(lax.rem(index, 2) + 1 + pipe, 2), index // 2)

    def back_copy(index):
        at = piece(index)
        return remote(
            back_out.at[:, at],
            back_in.at[:, at],
            z_send.at[0, index],
            z_recv.at[0, index],
            {"ctx": before},
        )

    def fwd_copy(index):
        at = piece(index)
        return remote(
            fwd_out.at[:, at],
            fwd_in.at[:, at],
            z_send.at[1, index],
            z_recv.at[1, index],
            {"ctx": after},
        )

    def x_copy(kind, src, dst, index, where):
        return remote(src, dst, x_send.at[kind, index], x_recv.at[kind, index], where)

    def pipe_copy(index):
        return x_copy(0, pipe_out.at[index], pipe_in.at[index], index, {"pipe": 1 - pipe})

    def half_copy(index):
        return x_copy(1, half_mine.at[index], half_other.at[index], index, {"dp": other_core})

    def lat_copy(index, side):
        at = columns(side, index)
        return x_copy(2, lat.at[:, at], lat.at[:, at], index, {"pipe": 1 - pipe})

    def lead_copy(index, turn, side):
        return remote(
            half_mine.at[index, pl.ds(0, 16), :],
            head_in.at[:, columns(side, index)],
            lead_send.at[index, turn],
            lead_recv.at[index, turn],
            {"ctx": before, "pipe": lax.rem(pipe + turn, 2)},
        )

    def rs_copy(index, step):
        to = lax.rem(ctx + step, n_ctx)
        return remote(
            conv_part.at[index, :, pl.ds(pl.multiple_of(to * share, share), share), :],
            conv_in.at[index, step],
            rs_send.at[index, step],
            rs_recv.at[index, step],
            {"ctx": to},
        )

    def project_away(index, carry):
        at = piece(index)
        fwd_out[:, at] = nn(dq_next[...], wt[0, half_width:, at]).astype(BF16)
        fwd_copy(index).start()
        back = nn(dk_prev[...], wt[1, :half_width, at])
        back = back + nn(dv_prev[...], wt[2, :half_width, at])
        back_out[:, at] = back.astype(BF16)
        back_copy(index).start()
        return carry

    lax.fori_loop(0, 4, project_away, 0)

    own_first(half_heads - 1)

    def own_late(index, carry):
        own_second(index)
        return carry

    lax.fori_loop(max(half_heads - 2, 0), half_heads, own_late, 0)

    def project_own(index):
        at = piece(index)
        own = nn(dq[...], wt[0, :, at]) + nn(dk[...], wt[1, :, at])
        return own + nn(dv[...], wt[2, :, at])

    def join_ctx(index, own):
        at = piece(index)
        fwd_copy(index).wait()
        back_copy(index).wait()
        return own + fwd_in[:, at].astype(F32) + back_in[:, at].astype(F32)

    def give(index):
        pipe_out[index] = join_ctx(2 * index, project_own(2 * index)).astype(BF16)
        pipe_copy(index).start()

    def settle(index, own):
        whole = join_ctx(2 * index + 1, own)
        pipe_copy(index).wait()
        latent = (whole + pipe_in[index].astype(F32)).astype(BF16)
        half_mine[index] = latent
        half_copy(index).start()
        lead_copy(index, 0, pipe).start()
        lead_copy(index, 1, pipe).start()
        lat[:, columns(pipe, index)] = latent
        lat_copy(index, pipe).start()

    def tap_grads(index):
        half_copy(index).wait()
        for i in range(2):
            conv_part[index, i] = (
                nn(taps_mine[i], half_mine[index]) + nn(taps_in[i], half_other[index])
            ).astype(BF16)

        def rs_start(step, carry):
            rs_copy(index, step).start()
            return carry

        lax.fori_loop(1, n_ctx, rs_start, 0)

    give(0)
    for i in range(2):
        taps_mine[i] = tap_rows(2 * core + i)
    give(1)
    own = project_own(1)
    for copy in taps_copies:
        copy.wait()
    settle(0, own)
    own = project_own(3)
    tap_grads(0)
    settle(1, own)
    tap_grads(1)

    for i in range(2):
        for turn in range(2):
            lead_copy(i, turn, pipe).wait_send()
            lead_copy(i, turn, lax.rem(pipe + turn, 2)).wait_recv()
        lat_copy(i, pipe).wait_send()
        lat_copy(i, 1 - pipe).wait_recv()
    swap.wait()
    ext[pl.ds(0, rows), :] = lat[...].astype(F32)
    ext[pl.ds(rows, 16), :] = head_in[...].astype(F32)

    def spread_tap(tap, shift):
        pos = col_pos + shift
        behind = (2, 1, 1, 0)[tap]
        live = (segment(pos - behind) == segment(pos)) & (pos < frames)
        masked = jnp.where(live, ext[pl.ds(shift, rows), :], 0.0).astype(BF16)
        return nt(masked, cw[tap])

    even = spread_tap(3, 0) + spread_tap(1, 1)
    odd = spread_tap(2, 1) + spread_tap(0, 2)
    for i in range(half // 128):
        at = slice(i * 128, (i + 1) * 128)
        spread[i, pl.ds(0, rows, stride=2), :] = even[:, at]
        spread[i, pl.ds(1, rows, stride=2), :] = odd[:, at]
        hid_out[:, at] = spread[i].astype(BF16)

    def dp_copy(index, turn, at):
        return remote(
            total.at[at, index],
            total.at[at, index],
            dp_send.at[index, turn],
            dp_recv.at[index, turn],
            {"dp": lax.rem(dp + turn, 4)},
        )

    def finish(index, carry):
        def rs_wait(step, carry):
            rs_copy(index, step).wait()
            return carry

        lax.fori_loop(1, n_ctx, rs_wait, 0)
        mine = conv_part[index, :, pl.ds(pl.multiple_of(ctx * share, share), share), :]
        arrived = jnp.sum(conv_in[index, 1:].astype(F32), axis=0)
        total[dp, index] = mine.astype(F32) + arrived
        for turn in range(1, 4):
            dp_copy(index, turn, dp).start()
        return carry

    lax.fori_loop(0, 2, finish, 0)
    for index in range(2):
        for turn in range(1, 4):
            dp_copy(index, turn, dp).wait_send()
            dp_copy(index, turn, lax.rem(dp + 4 - turn, 4)).wait_recv()
        at = slice(index * quarter, (index + 1) * quarter)
        for side in range(2):
            conv_out[2 * side : 2 * side + 2, :, at] = total[side, index] + total[2 + side, index]


def hand_on(hid_in, conv_in, hid_out, conv_out):
    hid_out[...] = hid_in[...]
    conv_out[...] = conv_in[...]


def body(queries, keys, values, outputs, out_grads, lengths, proj_weight, hidden, conv_weight):
    n_ctx = lax.axis_size("ctx")
    rows, width = queries.shape[1:]
    ch = proj_weight.shape[1]
    half = ch // 2
    half_width = width // 2
    half_heads = half_width // HEAD_DIM
    share = ch // n_ctx
    vmem = pltpu.VMEM
    dma = pltpu.SemaphoreType.DMA
    hidden_grad, conv_grad = pl.pallas_call(
        functools.partial(kernel, n_ctx),
        out_shape=(
            jax.ShapeDtypeStruct((2 * rows, half), BF16),
            jax.ShapeDtypeStruct((4, share, half), F32),
        ),
        in_specs=[pl.BlockSpec(memory_space=pltpu.SMEM)]
        + [pl.BlockSpec(memory_space=pl.ANY)] * 8,
        out_specs=(pl.BlockSpec(memory_space=pltpu.VMEM),) * 2,
        scratch_shapes=[vmem((rows, width), BF16)] * 5
        + [
            vmem((3, ch, width), BF16),
            vmem((3, width, ch), BF16),
            vmem((2 * rows, ch), BF16),
            vmem((4, half, ch), BF16),
        ]
        + [vmem((rows, half_width), BF16)] * 4
        + [vmem((rows, rows), F32)] * 3
        + [vmem((2 * half_heads, rows, rows), F32)]
        + [vmem((2 * half_heads, 8, rows), F32)]
        + [vmem((half_heads, 8, rows), F32)] * 3
        + [vmem((rows, width), BF16)] * 3
        + [vmem((rows, half_width), BF16)] * 3
        + [vmem((half_heads, HEAD_DIM, rows), F32)]
        + [vmem((rows, half_width), F32)] * 2
        + [vmem((rows, ch), BF16)] * 5
        + [vmem((2, rows, half // 2), BF16)] * 4
        + [
            vmem((rows + 16, ch), F32),
            vmem((16, ch), BF16),
            vmem((16, ch), BF16),
        ]
        + [vmem((2, ch, rows), BF16)] * 3
        + [
            vmem((half // 128, 2 * rows, 128), F32),
            vmem((2, 2, ch, half // 2), BF16),
            vmem((2, n_ctx, 2, share, half // 2), BF16),
            vmem((4, 2, 2, share, half // 2), F32),
            dma((8,)),
        ]
        + [dma((half_heads, 2))] * 4
        + [dma((half_heads,))] * 2
        + [dma((2, 4))] * 2
        + [dma((3, 2))] * 2
        + [dma((6,))] * 2
        + [dma((2, n_ctx))] * 2
        + [dma((2, 2))] * 2
        + [dma((2, 4))] * 2,
        compiler_params=pltpu.CompilerParams(
            collective_id=0, has_side_effects=True, vmem_limit_bytes=56 * 1024 * 1024
        ),
    )(
        lengths[0],
        queries[0],
        keys[0],
        values[0],
        outputs[0],
        out_grads[0],
        proj_weight,
        hidden[0],
        conv_weight,
    )
    hidden_grad, conv_grad = pl.pallas_call(
        hand_on,
        out_shape=(
            jax.ShapeDtypeStruct(hidden_grad.shape, BF16),
            jax.ShapeDtypeStruct(conv_grad.shape, F32),
        ),
        in_specs=[pl.BlockSpec(memory_space=pltpu.VMEM)] * 2,
        out_specs=(pl.BlockSpec(memory_space=pltpu.VMEM),) * 2,
    )(hidden_grad, conv_grad)
    return hidden_grad[None], conv_grad


def solution(mesh):
    placed = (
        P("dp", "ctx", "pipe"),
        P("dp", "ctx", "pipe"),
        P("dp", "ctx", "pipe"),
        P("dp", "ctx", "pipe"),
        P("dp", "ctx", "pipe"),
        P("dp", None),
        P(None, None, "pipe"),
        P("dp", "ctx", None),
        P(None, None, "pipe"),
    )
    return jax.shard_map(
        body,
        mesh=mesh,
        in_specs=placed,
        out_specs=(P("dp", "ctx", "pipe"), P(None, "ctx", "pipe")),
        check_vma=False,
    )
```
